512 devices in a mesh: row: 32 (over y, x), col: 16 (over z, core).
Axes of the slice: x: 4, y: 8, z: 8, core: 2. Of those that a mesh axis runs over, the one named last changes fastest.
Arguments:
- features: bfloat16 [65536, 512], P(('col', 'row')), may hold values from -6 to 6
- tile_vals: bfloat16 [32, 64, 256, 256], P('row', 'col')
- tile_rows: int32 [32, 64], P('row', 'col'), may hold values from 0 to 7, as said below
- tile_cols: int32 [32, 64], P('row', 'col'), may hold values from 0 to 15, as said below
- tile_count: int32 [32, 16], P('row', 'col'), may hold values from 1 to 4, as said below
- window: int32 [32, 2], P('row'), may hold values from 0 to 2048, as said below
- w_neigh: bfloat16 [512, 512], replicated, may hold values from -16 to 16
- w_self: bfloat16 [512, 512], replicated, may hold values from -0.25 to 0.25
- layer_bias: float32 [512], replicated, may hold values from -3 to 3
- cotangent: bfloat16 [65536, 512], P(('col', 'row')), may hold values from -6 to 6
Outputs:
- hidden_out: bfloat16 [65536, 512], P(('col', 'row'))
- grad_feat: bfloat16 [65536, 512], P(('col', 'row'))
- grad_neigh: bfloat16 [512, 512], replicated
- grad_self: bfloat16 [512, 512], replicated
- grad_bias: float32 [512], replicated
The draws below stay inside these ranges and needn't reach their ends.
Inputs may be any that keep to these rules, and one draw needn't show every extreme that they name: `tile_count`: each row block and column block has 2 to 4 live slots; some pair has exactly 4. `tile_rows`: within one row block and column block, slots m and m' name the same tile row only if m - m' is a multiple of 8. `tile_cols`: within one row block and column block, slots m and m' name the same tile column only if m - m' is a multiple of 16. window[r, 0] < window[r, 1]; some row block starts at 0 and some ends at 2048.
All inputs are finite; a program needn't handle non-finite values.
Results may differ from the reference program's by a relative error of at most 0.013.
Values may be sent and summed in bfloat16 or wider, within the bound.
A program may use at most 64 MiB of HBM per device.

```python
import math
import jax
import jax.numpy as jnp
from jax import lax

WIDTH = 512
TILE_EDGE = 256
ROWS_DEV = 128
SLOTS = 4
ROW_BLOCKS = 32
COL_BLOCKS = 16
COL_NODES = 4096
ROW_NODES = 2048
NODES = 65536


def draw_tile_vals(key, part):
    shape = (ROW_BLOCKS, COL_BLOCKS * SLOTS, TILE_EDGE, TILE_EDGE)
    block_pos = (jnp.arange(COL_BLOCKS * SLOTS, dtype=jnp.int32) // SLOTS).astype(jnp.float32)
    base = jax.random.uniform(key, shape, jnp.float32, 0.0, 1.0)
    factor = 1.0 + 2.0 * block_pos / max(COL_BLOCKS - 1, 1)
    return (base * factor[None, :, None, None]).astype(jnp.bfloat16)


def spread_tiles(key, count):
    keys = jax.random.split(key, ROW_BLOCKS * COL_BLOCKS)
    orders = jax.vmap(lambda one_key: jax.random.permutation(one_key, count))(keys)
    picks = jnp.arange(SLOTS, dtype=jnp.int32) % count
    chosen = orders[:, picks]
    return chosen.reshape(ROW_BLOCKS, COL_BLOCKS * SLOTS).astype(jnp.int32)


def draw_tile_rows(key, part):
    return spread_tiles(jax.random.fold_in(key, 11), ROW_NODES // TILE_EDGE)


def draw_tile_cols(key, part):
    return spread_tiles(jax.random.fold_in(key, 23), COL_NODES // TILE_EDGE)


def draw_tile_count(key, part):
    first, second, third = jax.random.split(key, 3)
    base = jax.random.randint(first, (ROW_BLOCKS, COL_BLOCKS), SLOTS // 2, SLOTS + 1)
    full = jax.random.randint(second, (ROW_BLOCKS, COL_BLOCKS), 0, 16) == 0
    chosen = jax.random.randint(third, (), 0, ROW_BLOCKS * COL_BLOCKS)
    flat_ids = jnp.arange(ROW_BLOCKS * COL_BLOCKS, dtype=jnp.int32).reshape(ROW_BLOCKS, COL_BLOCKS)
    return jnp.where(full | (flat_ids == chosen), SLOTS, base).astype(jnp.int32)


def draw_window(key, part):
    first, second, third, fourth = jax.random.split(key, 4)
    lower = jax.random.randint(first, (ROW_BLOCKS,), 0, ROW_NODES // 4)
    upper = ROW_NODES - jax.random.randint(second, (ROW_BLOCKS,), 0, ROW_NODES // 4)
    block_ids = jnp.arange(ROW_BLOCKS, dtype=jnp.int32)
    lower = jnp.where(block_ids == jax.random.randint(third, (), 0, ROW_BLOCKS), 0, lower)
    upper = jnp.where(block_ids == jax.random.randint(fourth, (), 0, ROW_BLOCKS), ROW_NODES, upper)
    return jnp.stack([lower, upper], axis=1).astype(jnp.int32)


def steps_of(own_key, shape, cuts, smallest, high):
    loudness, own = 1.0, jax.random.fold_in(own_key, 6)
    for dim, parts in cuts:
        draws = jnp.exp(jax.random.uniform(jax.random.fold_in(own, dim), (parts,), jnp.float32, smallest / len(cuts), high / len(cuts)))
        loudness = loudness * jnp.repeat(draws, shape[dim] // parts).reshape([-1 if axis == dim else 1 for axis in range(len(shape))])
    return loudness


def centred(key, dims, width, limit, cuts=(), kind=jnp.bfloat16):
    values = jax.random.normal(key, dims, jnp.float32) * width
    if len(cuts) > 0:
        values = steps_of(key, dims, cuts, -0.22, 0.18) * values
    return jnp.clip(values, min=-limit, max=limit).astype(kind)


def setup_inputs(seed: int = 0) -> dict:
    key_of = jax.random.split(jax.random.key(seed), 11)
    features = centred(key_of[0], (NODES, WIDTH), 1.0, 6.0, ((0, 512),))
    tile_vals = draw_tile_vals(jax.random.fold_in(key_of[10], 71), 0)
    tile_rows = draw_tile_rows(jax.random.fold_in(key_of[10], 71), 0)
    tile_cols = draw_tile_cols(jax.random.fold_in(key_of[10], 71), 0)
    tile_count = draw_tile_count(jax.random.fold_in(key_of[10], 71), 0)
    window = draw_window(jax.random.fold_in(key_of[10], 71), 0)
    w_neigh = centred(key_of[6], (WIDTH, WIDTH), 3.0, 16.0)
    w_self = centred(key_of[7], (WIDTH, WIDTH), WIDTH ** -0.5, 0.25)
    layer_bias = centred(key_of[8], (WIDTH,), 0.5, 3.0, (), jnp.float32)
    cotangent = centred(key_of[9], (NODES, WIDTH), 1.0, 6.0, ((0, 512),))
    return dict(features=features, tile_vals=tile_vals, tile_rows=tile_rows, tile_cols=tile_cols, tile_count=tile_count, window=window, w_neigh=w_neigh, w_self=w_self, layer_bias=layer_bias, cotangent=cotangent)


def reference(features, tile_vals, tile_rows, tile_cols, tile_count, window, w_neigh, w_self, layer_bias, cotangent):
    row_tiles = ROW_NODES // TILE_EDGE
    col_tiles = COL_NODES // TILE_EDGE
    highest = lax.Precision.HIGHEST
    node_grid = features.reshape(COL_BLOCKS, ROW_BLOCKS, ROWS_DEV, WIDTH)
    cot_grid = cotangent.reshape(COL_BLOCKS, ROW_BLOCKS, ROWS_DEV, WIDTH)
    panels = features.reshape(COL_BLOCKS, col_tiles, TILE_EDGE, WIDTH)
    slot_ids = jnp.arange(SLOTS, dtype=jnp.int32)
    row_ids = jnp.arange(row_tiles, dtype=jnp.int32)
    col_ids = jnp.arange(col_tiles, dtype=jnp.int32)
    local_rows = jnp.arange(ROW_NODES, dtype=jnp.int32)
    factor = 1.0 / math.sqrt(NODES)

    def one_block(carry, block_id):
        accum, sum_neigh, sum_self, sum_bias = carry
        tile_f32 = tile_vals[block_id].reshape(COL_BLOCKS, SLOTS, TILE_EDGE, TILE_EDGE).astype(jnp.float32)
        row_index = tile_rows[block_id].reshape(COL_BLOCKS, SLOTS)
        col_index = tile_cols[block_id].reshape(COL_BLOCKS, SLOTS)
        live_slots = (slot_ids[None, :] < tile_count[block_id][:, None]).astype(jnp.float32)
        row_hot = live_slots[:, :, None] * (row_index[:, :, None] == row_ids[None, None, :]).astype(jnp.float32)
        col_hot = live_slots[:, :, None] * (col_index[:, :, None] == col_ids[None, None, :]).astype(jnp.float32)
        inside = ((local_rows >= window[block_id, 0]) & (local_rows < window[block_id, 1])).astype(jnp.float32)
        pieces = jax.vmap(lambda panel_one, index_one: panel_one[index_one])(panels, col_index)
        products = jnp.einsum('cmij,cmjf->cmif', tile_f32, pieces.astype(jnp.float32), precision=highest)
        row_part = jnp.einsum('cmt,cmif->ctif', row_hot, products, precision=highest).reshape(COL_BLOCKS, ROW_NODES, WIDTH)
        row_part = row_part * inside[None, :, None]
        row_sums = lax.optimization_barrier(jnp.sum(tile_f32, axis=3))
        deg_part = jnp.einsum('cmt,cmi->cti', row_hot, row_sums, precision=highest).reshape(COL_BLOCKS, ROW_NODES)
        deg_part = deg_part * inside[None, :]
        aggregate = lax.optimization_barrier(jnp.sum(lax.optimization_barrier(row_part.astype(jnp.bfloat16)).astype(jnp.float32), axis=0))
        degree = lax.optimization_barrier(jnp.sum(lax.optimization_barrier(deg_part.astype(jnp.bfloat16)).astype(jnp.float32), axis=0))
        inverse = 1.0 / (1.0 + degree)
        neigh_rows = (aggregate * inverse[:, None]).astype(jnp.bfloat16)
        self_rows = node_grid[:, block_id].reshape(ROW_NODES, WIDTH)
        cot_rows = cot_grid[:, block_id].reshape(ROW_NODES, WIDTH)
        preact = jnp.dot(neigh_rows, w_neigh, preferred_element_type=jnp.float32)
        preact = preact + jnp.dot(self_rows, w_self, preferred_element_type=jnp.float32) + layer_bias
        sigmoid_z = jax.nn.sigmoid(preact)
        hidden_rows = (preact * sigmoid_z).astype(jnp.bfloat16)
        dpre = cot_rows.astype(jnp.float32) * (sigmoid_z * (1.0 + preact * (1.0 - sigmoid_z)))
        dpre_low = dpre.astype(jnp.bfloat16)
        sum_neigh = sum_neigh + jnp.dot(neigh_rows.T, dpre_low, preferred_element_type=jnp.float32)
        sum_self = sum_self + jnp.dot(self_rows.T, dpre_low, preferred_element_type=jnp.float32)
        sum_bias = sum_bias + lax.optimization_barrier(jnp.sum(dpre, axis=0))
        back_rows = jnp.dot(dpre_low, w_neigh.T, preferred_element_type=jnp.float32) * inverse[:, None] * inside[:, None]
        back_rows = back_rows.astype(jnp.bfloat16)
        picked = back_rows.reshape(row_tiles, TILE_EDGE, WIDTH)[row_index]
        backward = jnp.einsum('cmji,cmjf->cmif', tile_f32, picked.astype(jnp.float32), precision=highest)
        column_part = jnp.einsum('cmj,cmif->cjif', col_hot, backward, precision=highest).reshape(COL_BLOCKS, COL_NODES, WIDTH)
        accum = accum + lax.optimization_barrier(column_part.astype(jnp.bfloat16)).astype(jnp.float32)
        self_grad = jnp.dot(dpre_low, w_self.T, preferred_element_type=jnp.float32)
        outputs = (hidden_rows.reshape(COL_BLOCKS, ROWS_DEV, WIDTH), self_grad.reshape(COL_BLOCKS, ROWS_DEV, WIDTH))
        return ((accum, sum_neigh, sum_self, sum_bias), outputs)
    start = (jnp.zeros((COL_BLOCKS, COL_NODES, WIDTH), jnp.float32), jnp.zeros((WIDTH, WIDTH), jnp.float32), jnp.zeros((WIDTH, WIDTH), jnp.float32), jnp.zeros((WIDTH,), jnp.float32))
    carry, outputs = lax.scan(one_block, start, jnp.arange(ROW_BLOCKS, dtype=jnp.int32))
    accum, sum_neigh, sum_self, sum_bias = carry
    hidden_all, self_all = outputs
    hidden_out = jnp.transpose(hidden_all, (1, 0, 2, 3)).reshape(NODES, WIDTH)
    self_grad = jnp.transpose(self_all, (1, 0, 2, 3)).reshape(NODES, WIDTH)
    grad_feat = (self_grad + accum.reshape(NODES, WIDTH)).astype(jnp.bfloat16)
    grad_neigh = (sum_neigh * factor).astype(jnp.bfloat16)
    grad_self = (sum_self * factor).astype(jnp.bfloat16)
    grad_bias = sum_bias * factor
    return (hidden_out, grad_feat, grad_neigh, grad_self, grad_bias)
```

```python
import functools
import heapq
import math

import jax
import jax.numpy as jnp
from jax import lax
from jax.experimental import pallas as pl
from jax.experimental.pallas import tpu as pltpu
from jax.sharding import PartitionSpec as P

MESH = pl.DeviceIdType.MESH
BF = jnp.bfloat16
F32 = jnp.float32

NX = 4
ROUNDS = 2
ROWS = 128
HALF = ROWS // 2
LANES = 128
SEMS = 256
HOP = 1.5
UNIT = 0.65


def nn(a, b):
    return jnp.dot(a, b, preferred_element_type=F32)


def nt(a, b):
    return lax.dot_general(a, b, (((1,), (1,)), ((), ())), preferred_element_type=F32)


class Plan:
    def __init__(self):
        self.heap, self.count, self.now = [], 0, 0.0

    def spawn(self, chain, when):
        heapq.heappush(self.heap, (when, self.count, chain))
        self.count += 1

    def run(self):
        while self.heap:
            when, _, chain = heapq.heappop(self.heap)
            self.now = max(self.now, when)
            try:
                later = next(chain)
            except StopIteration:
                continue
            self.spawn(chain, later)


class Join:
    def __init__(self, count, then):
        self.count, self.then, self.when = count, then, 0.0

    def done(self, when):
        self.count -= 1
        self.when = max(self.when, when)
        if self.count == 0:
            self.then(self.when)


class Links:
    def __init__(self, send, recv):
        self.send, self.recv, self.used, self.sent = send, recv, 0, []

    def start(self, src, dst, device):
        at = self.used
        self.used += 1
        copy = pltpu.make_async_remote_copy(
            src_ref=src,
            dst_ref=dst,
            send_sem=self.send.at[at],
            recv_sem=self.recv.at[at],
            device_id=device,
            device_id_type=MESH,
        )
        copy.start()
        self.sent.append(copy)
        return copy

    def finish(self):
        for copy in self.sent:
            copy.wait_send()


class Direct:
    def __init__(self, links, size, me, device, src, dst):
        self.links, self.size, self.me = links, size, me
        self.device, self.src, self.dst = device, src, dst
        self.base = links.used
        links.used += size - 1
        links.sent.append(self)

    def copy(self, step):
        other = lax.rem(self.me + step, self.size)
        return pltpu.make_async_remote_copy(
            src_ref=self.src(other),
            dst_ref=self.dst(self.me),
            send_sem=self.links.send.at[self.base + step - 1],
            recv_sem=self.links.recv.at[self.base + step - 1],
            device_id=self.device(other),
            device_id_type=MESH,
        )

    def start(self):
        @pl.loop(1, self.size)
        def _(step):
            self.copy(step).start()

    def wait_recv(self):
        @pl.loop(1, self.size)
        def _(step):
            self.copy(step).wait_recv()

    def wait_send(self):
        @pl.loop(1, self.size)
        def _(step):
            self.copy(step).wait_send()


def gather_chain(links, way, size, me, block, device, begin, hop, done):
    steps = size // 2
    clock, copy = begin, None
    for step in range(1, steps + 1):
        if copy is not None:
            clock += hop
            yield clock
            copy.wait_recv()
        owner = lax.rem(me - way * (step - 1) + size, size)
        part = None if step < steps else (0 if way > 0 else 1)
        ref = block(owner, part)
        copy = links.start(ref, ref, device(lax.rem(me + way + size, size)))
    clock += hop
    yield clock
    copy.wait_recv()
    done(clock)


def scatter_chain(links, way, size, me, block, slot, add, device, begin, hop, done):
    steps = size // 2
    clock, copy = begin, None
    half = 0 if way > 0 else 1
    for step in range(1, steps + 1):
        owner = lax.rem(me + way * (steps - step + 1) + size, size)
        part = half if step == 1 else None
        if copy is not None:
            clock += hop
            yield clock
            copy.wait_recv()
            was = half if step == 2 else None
            add(block(owner, was), slot(step - 1, was))
        copy = links.start(
            block(owner, part), slot(step, part), device(lax.rem(me + way + size, size))
        )
    clock += hop
    yield clock
    copy.wait_recv()
    done(clock)


def add_into(to, frm):
    to[...] = to[...] + frm[...]


def layer(
    sizes,
    feat,
    tiles,
    tile_rows,
    tile_cols,
    tile_count,
    window,
    w_neigh,
    w_self,
    bias,
    cot,
    hidden_out,
    gfeat_out,
    gneigh_out,
    gself_out,
    gbias_out,
    *scratch,
):
    names = list(scratch)

    def take():
        return names.pop(0)

    NY, NZ, SLOTS, EDGE, WIDTH = sizes
    NC = 2 * NZ
    XH = NX // 2
    CW = 2 * LANES
    panel = [take() for _ in range(ROUNDS)]
    part = [take() for _ in range(ROUNDS)]
    pair = [take() for _ in range(ROUNDS)]
    zslot = [take() for _ in range(ROUNDS)]
    back = [take() for _ in range(ROUNDS)]
    colp = [take() for _ in range(ROUNDS)]
    ry0 = [take() for _ in range(ROUNDS)]
    rx0 = [take() for _ in range(ROUNDS)]
    rx1 = [take() for _ in range(ROUNDS)]
    ry1 = [take() for _ in range(ROUNDS)]
    tile = take()
    turned = take()
    featv, cotv, wnv, wsv = take(), take(), take(), take()
    deg_own, deg_all = take(), take()
    own_in, inv = take(), take()
    pre = take()
    selfg = take()
    lhs, lhs_in = take(), take()
    dlow, dlow_in = take(), take()
    dbias, dbias_in = take(), take()
    ez, ez_in = take(), take()
    bz_in = take()
    ey, ey_in = take(), take()
    ex, ex_in = take(), take()
    ag = take()
    grads = take()
    hid, gft = take(), take()
    send, recv, local = take(), take(), take()
    assert not names

    r, c = lax.axis_index("row"), lax.axis_index("col")
    y, x = r // NX, lax.rem(r, NX)
    z, k = c // 2, lax.rem(c, 2)
    mate = 1 - k

    def at_x(i):
        return {"row": y * NX + i}

    def at_y(i):
        return {"row": i * NX + x}

    def at_z(i):
        return {"col": i * 2 + k}

    def at_c(i):
        return {"col": i}

    partner = {"col": z * 2 + mate}

    loads = []

    def load(src, dst):
        copy = pltpu.make_async_copy(src, dst, local.at[len(loads)])
        copy.start()
        loads.append(copy)
        return copy

    own = []
    for q in range(ROUNDS):
        for h in range(2):
            cols = pl.ds((2 * q + h) * LANES, LANES)
            own.append(load(feat.at[:, cols], panel[q].at[h, y, x]))
    tile_load = load(tiles.at[0], tile.at[pl.ds(0, SLOTS)])
    feat_load = load(feat, featv)
    ws_load = load(w_self, wsv)
    wn_load = load(w_neigh, wnv)
    cot_load = load(cot, cotv)

    barrier = pltpu.get_barrier_semaphore()

    @pl.loop(1, NX)
    def _(i):
        pl.semaphore_signal(barrier, inc=1, device_id=at_x(lax.rem(x + i, NX)), device_id_type=MESH)

    @pl.loop(1, NY)
    def _(i):
        pl.semaphore_signal(barrier, inc=1, device_id=at_y(lax.rem(y + i, NY)), device_id_type=MESH)

    @pl.loop(1, NC)
    def _(i):
        pl.semaphore_signal(barrier, inc=1, device_id=at_c(lax.rem(c + i, NC)), device_id_type=MESH)

    pl.semaphore_wait(barrier, NX + NY + NC - 3)

    links, plan = Links(send, recv), Plan()
    for copy in own:
        copy.wait()

    lo, hi = window[0, 0], window[0, 1]
    count = tile_count[0, 0]
    slot_row = [tile_rows[0, m] for m in range(SLOTS)]
    slot_col = [tile_cols[0, m] for m in range(SLOTS)]

    def slot_of(ids, want):
        found = jnp.int32(SLOTS)
        for m in range(SLOTS):
            found = jnp.where((ids[m] == want) & (m < count), m, found)
        return found

    def value_at(ids, m):
        found = ids[0]
        for i in range(1, SLOTS):
            found = jnp.where(m == i, ids[i], found)
        return found

    def rows2(ref, *lead):
        return lambda owner, p: (
            ref.at[(*lead, owner)]
            if p is None
            else ref.at[(*lead, owner, pl.ds(HALF * p, HALF))]
        )

    def gather0(q, begin):
        def rows_then(when):
            end = Join(2, lambda t: ready_a[q].done(t))
            for way in (1, -1):

                def block(o, p):
                    if p is None:
                        return panel[q].at[0, o]
                    return panel[q].at[0, o, pl.ds(XH * p, XH)]

                plan.spawn(
                    gather_chain(links, way, NY, y, block, at_y, when, HOP + NX * UNIT, end.done),
                    when,
                )

        mid = Join(2, rows_then)
        for way in (1, -1):
            plan.spawn(
                gather_chain(links, way, NX, x, rows2(panel[q], 0, y), at_x, begin, HOP + UNIT, mid.done),
                begin,
            )

    def gather1(q, begin):
        def cols_then(when):
            end = Join(2, lambda t: ready_a[q].done(t))
            for way in (1, -1):

                def block(o, p):
                    if p is None:
                        return panel[q].at[1, :, o]
                    return panel[q].at[1, pl.ds(NY // 2 * p, NY // 2), o]

                plan.spawn(
                    gather_chain(links, way, NX, x, block, at_x, when, HOP + NY * UNIT, end.done),
                    when,
                )

        def block(o, p):
            if p is None:
                return panel[q].at[1, o, x]
            return panel[q].at[1, o, x, pl.ds(HALF * p, HALF)]

        mid = Join(2, cols_then)
        for way in (1, -1):
            plan.spawn(
                gather_chain(links, way, NY, y, block, at_y, begin, HOP + UNIT, mid.done),
                begin,
            )

    def prepare(when):
        yield when
        tile_load.wait()
        tile[SLOTS] = jnp.zeros((EDGE, EDGE), BF)

        @pl.loop(0, SLOTS + 1)
        def _(m):
            turned[m] = tile[m].T

        lane = lax.broadcasted_iota(jnp.int32, (8, EDGE), 1)

        @pl.loop(0, NZ)
        def _(t):
            total = nn(jnp.ones((8, EDGE), BF), turned[slot_of(slot_row, t)])
            at = lane + t * EDGE
            total = jnp.where((at >= lo) & (at < hi), total, 0.0)
            deg_own[2 * t] = total[:, :ROWS]
            deg_own[2 * t + 1] = total[:, ROWS:]

        deg_all[c] = deg_own[c]
        degree.start()
        yield when + 0.5
        feat_load.wait()
        ws_load.wait()
        pre[...] = nn(featv[...], wsv[...]) + bias[...]
        lhs[1] = featv[...]
        at = lax.broadcasted_iota(jnp.int32, (ROWS, LANES), 0) + c * ROWS
        own_in[...] = jnp.where((at >= lo) & (at < hi), 1.0, 0.0)
        yield when + 12.0
        degree.wait_recv()
        total = deg_all[0]
        for i in range(1, NC):
            total = total + deg_all[i]
        inverse = 1.0 / (1.0 + total)
        inv[...] = jnp.tile(inverse, (ROWS // 8, 1)).T
        wn_load.wait()
        cot_load.wait()

    degree = Direct(links, NC, c, at_c, lambda o: deg_own.at[o], lambda i: deg_all.at[i])

    def forward(q, when):
        yield when

        @pl.loop(0, NZ)
        def _(t):
            m = slot_of(slot_row, t)
            j = value_at(slot_col, m)
            yy, xx = j // XH, lax.rem(j, XH) * 2
            left = panel[q][0, yy, pl.ds(xx, 2)].reshape(EDGE, LANES)
            right = panel[q][1, yy, pl.ds(xx, 2)].reshape(EDGE, LANES)
            out = nn(tile[m], jnp.concatenate([left, right], axis=1))
            at = lax.broadcasted_iota(jnp.int32, (EDGE, CW), 0) + t * EDGE
            out = jnp.where((at >= lo) & (at < hi), out, 0.0).astype(BF)
            part[q][0, t] = out[:ROWS]
            part[q][1, t] = out[ROWS:]

        swap = links.start(part[q].at[mate], pair[q], partner)
        when = max(when, plan.now) + 4.0
        yield when
        swap.wait_recv()

        @pl.loop(0, NZ)
        def _(t):
            pair[q][t] = pair[q][t] + part[q][k, t]

        end = Join(2, lambda t: ready_b.done(t))
        for way in (1, -1):
            w = 0 if way > 0 else 1

            def slot(step, p, w=w):
                if p is None:
                    return zslot[q].at[w, step - 1]
                return zslot[q].at[w, step - 1, pl.ds(HALF * p, HALF)]

            plan.spawn(
                scatter_chain(
                    links, way, NZ, z, rows2(pair[q]), slot, add_into, at_z, when, HOP + 2 * UNIT, end.done
                ),
                when,
            )

    def middle(when):
        yield when
        last = NZ // 2 - 1
        wide = jnp.concatenate([inv[...], inv[...]], axis=1)
        for q in range(ROUNDS):
            total = pair[q][z].astype(F32) + zslot[q][0, last].astype(F32) + zslot[q][1, last].astype(F32)
            low = (total * wide).astype(BF)
            lhs[0, :, q * CW : (q + 1) * CW] = low
            pre[...] += nn(low, wnv[q * CW : (q + 1) * CW, :])
        value = pre[...]
        s = jax.nn.sigmoid(value)
        hid[...] = (value * s).astype(BF)
        hidden_store.start()
        dpre = cotv[...].astype(F32) * (s * (1.0 + value * (1.0 - s)))
        low = dpre.astype(BF)
        dlow[...] = low
        scale = wide * jnp.concatenate([own_in[...], own_in[...]], axis=1)
        for q in range(ROUNDS):
            out = nt(low, wnv[q * CW : (q + 1) * CW, :]) * scale
            back[q][z, k] = out.astype(BF)
        when = max(when, plan.now) + 2.0
        for q in range(ROUNDS):
            spread(q, when + 0.1 * q)
        total = dpre[0:8]
        for i in range(1, ROWS // 8):
            total = total + dpre[8 * i : 8 * i + 8]
        dbias[...] = total
        plan.spawn(gradients(when), when + 0.5)
        yield when + 1.0
        selfg[...] = nt(dlow[...], wsv[...])

    hidden_store = pltpu.make_async_copy(hid, hidden_out, local.at[9])

    def spread(q, when):
        def chain(way, begin, done):
            steps = NZ // 2
            clock, copy = begin, None
            for step in range(1, steps + 2):
                owner = lax.rem(z - way * (step - 1) + NZ, NZ)
                was = None if step <= steps else (0 if way > 0 else 1)
                now = None if step < steps else (0 if way > 0 else 1)
                if copy is not None:
                    clock += HOP + 2 * UNIT
                    yield clock
                    copy.wait_recv()
                if step <= steps:
                    ref = block(owner, now)
                    copy = links.start(ref, ref, at_z(lax.rem(z + way + NZ, NZ)))
                if step > 1 or way > 0:
                    ref = block(owner, was)
                    mates.append(links.start(ref, ref, partner))
            done(clock)

        def block(o, p):
            if p is None:
                return back[q].at[o, k]
            return back[q].at[o, k, pl.ds(HALF * p, HALF)]

        mates = []
        end = Join(2, lambda t: plan.spawn(backward(q, t + HOP, mates), t + HOP))
        for way in (1, -1):
            plan.spawn(chain(way, when, end.done), when)

    def backward(q, when, mates):
        yield when
        for copy in mates:
            copy.wait_recv()

        @pl.loop(0, NY * XH)
        def _(j):
            m = slot_of(slot_col, j)
            t = value_at(slot_row, m)
            out = nn(turned[m], back[q][t].reshape(EDGE, CW)).astype(BF)
            yy, xx = j // XH, lax.rem(j, XH) * 2
            for h in range(2):
                for i in range(2):
                    colp[q][h, yy, xx + i] = out[i * ROWS : (i + 1) * ROWS, h * LANES : (h + 1) * LANES]

        when = max(when, plan.now) + 2.0
        scatter0(q, when)
        scatter1(q, when)

    def scatter0(q, begin):
        last_y, last_x = NY // 2 - 1, NX // 2 - 1

        def finish(when):
            write(q, 0, rx0[q][0, last_x], rx0[q][1, last_x])
            ready_d.done(when)

        def then(when):
            for w in range(2):
                add_into(colp[q].at[0, y], ry0[q].at[w, last_y])
            end = Join(2, finish)
            for way in (1, -1):
                w = 0 if way > 0 else 1

                def slot(step, p, w=w):
                    if p is None:
                        return rx0[q].at[w, step - 1]
                    return rx0[q].at[w, step - 1, pl.ds(HALF * p, HALF)]

                plan.spawn(
                    scatter_chain(
                        links, way, NX, x, rows2(colp[q], 0, y), slot, add_into, at_x, when, HOP + UNIT, end.done
                    ),
                    when,
                )

        mid = Join(2, then)
        for way in (1, -1):
            w = 0 if way > 0 else 1

            def block(o, p):
                if p is None:
                    return colp[q].at[0, o]
                return colp[q].at[0, o, pl.ds(XH * p, XH)]

            def slot(step, p, w=w):
                if p is None:
                    return ry0[q].at[w, step - 1]
                return ry0[q].at[w, step - 1, pl.ds(XH * p, XH)]

            plan.spawn(
                scatter_chain(links, way, NY, y, block, slot, add_into, at_y, begin, HOP + NX * UNIT, mid.done),
                begin,
            )

    def scatter1(q, begin):
        last_y, last_x = NY // 2 - 1, NX // 2 - 1

        def finish(when):
            write(q, 1, ry1[q][0, last_y], ry1[q][1, last_y])
            ready_d.done(when)

        def then(when):
            for w in range(2):
                add_into(colp[q].at[1, :, x], rx1[q].at[w, last_x])
            end = Join(2, finish)
            for way in (1, -1):
                w = 0 if way > 0 else 1

                def block(o, p):
                    if p is None:
                        return colp[q].at[1, o, x]
                    return colp[q].at[1, o, x, pl.ds(HALF * p, HALF)]

                def slot(step, p, w=w):
                    if p is None:
                        return ry1[q].at[w, step - 1]
                    return ry1[q].at[w, step - 1, pl.ds(HALF * p, HALF)]

                plan.spawn(
                    scatter_chain(links, way, NY, y, block, slot, add_into, at_y, when, HOP + UNIT, end.done),
                    when,
                )

        mid = Join(2, then)
        for way in (1, -1):
            w = 0 if way > 0 else 1
            deep = NY // 2

            def block(o, p):
                if p is None:
                    return colp[q].at[1, :, o]
                return colp[q].at[1, pl.ds(deep * p, deep), o]

            def slot(step, p, w=w):
                if p is None:
                    return rx1[q].at[w, step - 1]
                return rx1[q].at[w, step - 1, pl.ds(deep * p, deep)]

            plan.spawn(
                scatter_chain(links, way, NX, x, block, slot, add_into, at_x, begin, HOP + NY * UNIT, mid.done),
                begin,
            )

    def write(q, h, one, two):
        cols = slice((2 * q + h) * LANES, (2 * q + h + 1) * LANES)
        total = colp[q][h, y, x].astype(F32) + one.astype(F32) + two.astype(F32)
        gft[:, cols] = (total + selfg[:, cols]).astype(BF)

    def gradients(when):
        yield when
        swaps = [
            links.start(lhs.at[mate], lhs_in, partner),
            links.start(dlow, dlow_in, partner),
            links.start(dbias, dbias_in, partner),
        ]
        yield when + 4.0
        for copy in swaps:
            copy.wait_recv()
        bz_in[z] = dbias[...] + dbias_in[...]
        both = jnp.concatenate([dlow[...], dlow_in[...]], axis=0)
        deep = WIDTH // NZ

        wide = WIDTH // 4
        for i in range(4):
            cut = slice(i * wide, (i + 1) * wide)
            left = jnp.concatenate([lhs[k, :, cut], lhs_in[:, cut]], axis=0)
            out = nn(left.T, both)
            for j in range(wide // deep):
                ez[i * (wide // deep) + j] = out[j * deep : (j + 1) * deep].astype(BF)
        ez_in[z] = ez[z]
        sum_z.start()
        bias_z.start()
        yield when + 16.0
        sum_z.wait_recv()
        bias_z.wait_recv()
        total = ez_in[0].astype(F32)
        for i in range(1, NZ):
            total = total + ez_in[i].astype(F32)
        low = bz_in[0]
        for i in range(1, NZ):
            low = low + bz_in[i]
        for i in range(NY):
            ey[i, 0:8] = total[8 * i : 8 * i + 8]
            ey[i, 8:16] = low
        ey_in[y] = ey[y]
        sum_y.start()
        yield when + 21.0
        sum_y.wait_recv()
        total = ey_in[0]
        for i in range(1, NY):
            total = total + ey_in[i]
        ex[...] = total
        ex_in[x] = total
        sum_x.start()
        yield when + 26.0
        sum_x.wait_recv()
        total = ex_in[0]
        for i in range(1, NX):
            total = total + ex_in[i]
        total = total * factor
        gbias_out[...] = jnp.sum(total[8:16], axis=0, keepdims=True)
        ag[y] = total[0:8]
        all_y.start()
        yield when + 31.0
        all_y.wait_recv()
        grads[k, z] = jnp.concatenate([ag[i] for i in range(NY)], axis=0).astype(BF)
        all_z.start()
        yield when + 42.0
        all_z.wait_recv()
        last = links.start(grads.at[k], grads.at[k], partner)
        yield when + 45.0
        last.wait_recv()
        ready_e.done(when + 45.0)

    factor = 1.0 / math.sqrt(ROWS * NY * NX * NC)
    sum_z = Direct(links, NZ, z, at_z, lambda o: ez.at[o], lambda i: ez_in.at[i])
    bias_z = Direct(links, NZ, z, at_z, lambda o: bz_in.at[z], lambda i: bz_in.at[i])
    sum_y = Direct(links, NY, y, at_y, lambda o: ey.at[o], lambda i: ey_in.at[i])
    sum_x = Direct(links, NX, x, at_x, lambda o: ex, lambda i: ex_in.at[i])
    all_y = Direct(links, NY, y, at_y, lambda o: ag.at[y], lambda i: ag.at[i])
    all_z = Direct(links, NZ, z, at_z, lambda o: grads.at[k, z], lambda i: grads.at[k, i])

    ready_a = [Join(2, lambda t, q=q: plan.spawn(forward(q, t), t)) for q in range(ROUNDS)]
    ready_b = Join(ROUNDS, lambda t: plan.spawn(middle(t), t))
    ready_d = Join(2 * ROUNDS, lambda t: None)
    ready_e = Join(1, lambda t: None)
    for q in range(ROUNDS):
        gather0(q, 0.05 * q)
        gather1(q, 0.05 * q)
    plan.spawn(prepare(0.5), 0.5)
    plan.run()

    stores = [
        pltpu.make_async_copy(gft, gfeat_out, local.at[10]),
        pltpu.make_async_copy(grads.at[0], gneigh_out, local.at[11]),
        pltpu.make_async_copy(grads.at[1], gself_out, local.at[12]),
    ]
    for copy in stores:
        copy.start()
    links.finish()
    hidden_store.wait()
    for copy in stores:
        copy.wait()


def on_device(
    features, tile_vals, tile_rows, tile_cols, tile_count, window, w_neigh, w_self, layer_bias, cotangent
):
    rows, width = features.shape
    slots, edge = tile_vals.shape[1:3]
    ny = lax.axis_size("row") // NX
    nz = lax.axis_size("col") // 2
    nc = 2 * nz

    def vmem(*shape, dtype=BF):
        return pltpu.VMEM(shape, dtype)

    cw = 2 * LANES
    each = [
        (2, ny, NX, ROWS, LANES),
        (2, nz, ROWS, cw),
        (nz, ROWS, cw),
        (2, nz // 2, ROWS, cw),
        (nz, 2, ROWS, cw),
        (2, ny, NX, ROWS, LANES),
        (2, ny // 2, NX, ROWS, LANES),
        (2, NX // 2, ROWS, LANES),
        (2, NX // 2, ny, ROWS, LANES),
        (2, ny // 2, ROWS, LANES),
    ]
    deep = width // nz
    scratch = [vmem(*shape) for shape in each for _ in range(ROUNDS)]
    scratch += [vmem(slots + 1, edge, edge)] * 2
    scratch += [vmem(rows, width), vmem(rows, width), vmem(width, width), vmem(width, width)]
    scratch += [vmem(nc, 8, ROWS, dtype=F32)] * 2
    scratch += [vmem(ROWS, LANES, dtype=F32)] * 2
    scratch += [vmem(rows, width, dtype=F32)] * 2
    scratch += [vmem(2, rows, width), vmem(rows, width)]
    scratch += [vmem(rows, width)] * 2
    scratch += [vmem(8, width, dtype=F32)] * 2
    scratch += [vmem(nz, deep, width)] * 2
    scratch += [vmem(nz, 8, width, dtype=F32)]
    scratch += [vmem(ny, 16, width, dtype=F32)] * 2
    scratch += [vmem(16, width, dtype=F32), vmem(NX, 16, width, dtype=F32)]
    scratch += [vmem(ny, 8, width, dtype=F32)]
    scratch += [vmem(2, nz, deep, width)]
    scratch += [vmem(rows, width)] * 2
    scratch += [pltpu.SemaphoreType.DMA((SEMS,))] * 2 + [pltpu.SemaphoreType.DMA((16,))]
    anywhere = pl.BlockSpec(memory_space=pl.ANY)
    small = pl.BlockSpec(memory_space=pltpu.SMEM)
    fast = pl.BlockSpec(memory_space=pltpu.VMEM)
    sizes = (ny, nz, slots, edge, width)
    hidden, gfeat, gneigh, gself, gbias = pl.pallas_call(
        functools.partial(layer, sizes),
        out_shape=(
            jax.ShapeDtypeStruct((rows, width), BF),
            jax.ShapeDtypeStruct((rows, width), BF),
            jax.ShapeDtypeStruct((nz, deep, width), BF),
            jax.ShapeDtypeStruct((nz, deep, width), BF),
            jax.ShapeDtypeStruct((1, width), F32),
        ),
        in_specs=[anywhere, anywhere, small, small, small, small, anywhere, anywhere, fast, anywhere],
        out_specs=(anywhere, anywhere, anywhere, anywhere, fast),
        scratch_shapes=scratch,
        compiler_params=pltpu.CompilerParams(
            collective_id=0, has_side_effects=True, vmem_limit_bytes=48 * 1024 * 1024
        ),
    )(
        features,
        tile_vals,
        tile_rows,
        tile_cols,
        tile_count,
        window,
        w_neigh,
        w_self,
        layer_bias.reshape(1, width),
        cotangent,
    )
    return hidden, gfeat, gneigh.reshape(width, width), gself.reshape(width, width), gbias.reshape(width)


def solution(mesh):
    in_specs = (
        P(("col", "row"), None),
        P("row", "col", None, None),
        P("row", "col"),
        P("row", "col"),
        P("row", "col"),
        P("row", None),
        P(),
        P(),
        P(),
        P(("col", "row"), None),
    )
    out_specs = (P(("col", "row"), None), P(("col", "row"), None), P(), P(), P())
    return jax.shard_map(
        on_device, mesh=mesh, in_specs=in_specs, out_specs=out_specs, check_vma=False
    )
```

```python
import functools
import heapq
import math

import jax
import jax.numpy as jnp
from jax import lax
from jax.experimental import pallas as pl
from jax.experimental.pallas import tpu as pltpu
from jax.sharding import PartitionSpec as P

MESH = pl.DeviceIdType.MESH
BF = jnp.bfloat16
F32 = jnp.float32

NX = 4
FWD = ((256, False), (256, False),)
BWD = ((256, False), (256, False),)
STAGGER = 0
ROWS = 128
HALF = ROWS // 2
LANES = 128
SEMS = 400
VMEM_LIMIT = 63 * 1024 * 1024
LINK_RATE, HOP = 88e3, 1.6
CORE_RATE, CORE_HOP = 350e3, 0.9
ISSUE = 0.07
PLANE = 3.5


def nn(a, b):
    return jnp.dot(a, b, preferred_element_type=F32)


def nt(a, b):
    return lax.dot_general(a, b, (((1,), (1,)), ((), ())), preferred_element_type=F32)


class Plan:
    def __init__(self):
        self.heap, self.count, self.now, self.idle = [], 0, 0.0, []

    def spawn(self, chain, when):
        heapq.heappush(self.heap, (when, self.count, chain))
        self.count += 1

    def later(self, cost, work):
        self.idle.append((cost, work))

    def flush(self):
        while self.idle:
            cost, work = self.idle.pop(0)
            work()
            self.now += cost

    def run(self):
        while self.heap or self.idle:
            if self.idle and (not self.heap or self.heap[0][0] > self.now + self.idle[0][0]):
                cost, work = self.idle.pop(0)
                work()
                self.now += cost
                continue
            when, _, chain = heapq.heappop(self.heap)
            self.now = max(self.now, when)
            try:
                self.spawn(chain, next(chain))
            except StopIteration:
                pass


class Join:
    def __init__(self, count, then):
        self.count, self.then = count, then

    def done(self):
        self.count -= 1
        if self.count == 0:
            self.then()


class Links:
    def __init__(self, plan, send, recv):
        self.plan, self.send, self.recv, self.used, self.sent = plan, send, recv, 0, []
        self.free = {}

    def start(self, src, dst, device, link, hops=1):
        at = self.used
        self.used += 1
        copy = pltpu.make_async_remote_copy(
            src_ref=src,
            dst_ref=dst,
            send_sem=self.send.at[at],
            recv_sem=self.recv.at[at],
            device_id=device,
            device_id_type=MESH,
        )
        copy.start()
        self.sent.append(copy)
        size = math.prod(src.shape) * src.dtype.itemsize
        rate, hop = (CORE_RATE, CORE_HOP) if link == "core" else (LINK_RATE / 2, HOP)
        self.plan.now += ISSUE
        ready = max(self.plan.now, self.free.get(link, 0.0)) + hops * size / rate
        self.free[link] = ready
        return copy, ready + hop + 0.3 * (hops - 1)

    def finish(self):
        for copy in self.sent:
            copy.wait_send()


class Direct:
    def __init__(self, links, size, me, device, src, dst):
        self.links, self.size, self.me = links, size, me
        self.device, self.src, self.dst = device, src, dst
        self.base = links.used
        links.used += size - 1
        links.sent.append(self)

    def copy(self, step):
        other = lax.rem(self.me + step, self.size)
        return pltpu.make_async_remote_copy(
            src_ref=self.src(other),
            dst_ref=self.dst(self.me),
            send_sem=self.links.send.at[self.base + step - 1],
            recv_sem=self.links.recv.at[self.base + step - 1],
            device_id=self.device(other),
            device_id_type=MESH,
        )

    def start(self):
        @pl.loop(1, self.size)
        def _(step):
            self.copy(step).start()

        self.links.plan.now += ISSUE * self.size

    def wait_recv(self):
        @pl.loop(1, self.size)
        def _(step):
            self.copy(step).wait_recv()

    def wait_send(self):
        @pl.loop(1, self.size)
        def _(step):
            self.copy(step).wait_send()


def gather_chain(links, axis, way, size, me, block, device, done, pass_on=None):
    steps, held = size // 2, None
    half = 0 if way > 0 else 1
    for step in range(1, steps + 2):
        owner = lax.rem(me - way * (step - 1) + size, size)
        if held is not None:
            yield held[1]
            held[0].wait_recv()
        if step <= steps:
            ref = block(owner, None if step < steps else half)
            held = links.start(ref, ref, device(lax.rem(me + way + size, size)), (axis, way))
        if pass_on is not None and (step > 1 or way > 0):
            pass_on(block(owner, None if step <= steps else half))
    done()


def scatter_chain(links, axis, way, size, me, block, slot, device, done):
    steps, held = size // 2, None
    half = 0 if way > 0 else 1
    for step in range(1, steps + 1):
        owner = lax.rem(me + way * (steps - step + 1) + size, size)
        part = half if step == 1 else None
        if held is not None:
            yield held[1]
            held[0].wait_recv()
            was = half if step == 2 else None
            add_into(block(owner, was), slot(step - 1, was))
            links.plan.now += 0.2
        held = links.start(
            block(owner, part), slot(step, part), device(lax.rem(me + way + size, size)), (axis, way)
        )
    yield held[1]
    held[0].wait_recv()
    done()


def add_into(to, frm):
    to[...] = to[...] + frm[...]


def layer(
    sizes,
    feat,
    tiles,
    rows_in,
    cols_in,
    count_in,
    window_in,
    w_neigh,
    w_self,
    bias_in,
    cot,
    hidden_out,
    gfeat_out,
    grads_out,
    gbias_out,
    *scratch,
):
    names = list(scratch)

    def take():
        return names.pop(0)

    NY, NZ, SLOTS, EDGE, WIDTH = sizes
    NC, NR = 2 * NZ, NX * NY
    XH = NX // 2
    DEEP = WIDTH // NZ
    fwd, bwd = range(len(FWD)), range(len(BWD))
    fwd_at = [sum(w for w, _ in FWD[:q]) for q in fwd]
    bwd_at = [sum(w for w, _ in BWD[:q]) for q in bwd]
    panel = [take() for _ in fwd]
    part = [take() for _ in fwd]
    pair = [take() for _ in fwd]
    zslot = [take() for _ in fwd]
    prod = [take() for _ in fwd]
    back = [take() for _ in bwd]
    back_prod = [take() for _ in bwd]
    colp = [take() for _ in bwd]
    ry0 = [take() for _ in bwd]
    rx0 = [take() for _ in bwd]
    rx1 = [take() for _ in bwd]
    ry1 = [take() for _ in bwd]
    tile = take()
    turned = take()
    featv, cotv, wnv, wsv = take(), take(), take(), take()
    bias = take()
    deg_own, deg_all = take(), take()
    own_in, inv = take(), take()
    pre = take()
    selfg = take()
    lhs, lhs_in = take(), take()
    dlow, dlow_in = take(), take()
    dbias, dbias_in = take(), take()
    ez, ez_in = take(), take()
    bz_in = take()
    ex, ex_in = take(), take()
    ey, ey_in = take(), take()
    ag = take()
    grads = take()
    hid, gft, gb = take(), take(), take()
    tile_rows, tile_cols, tile_count, window = take(), take(), take(), take()
    send, recv, local = take(), take(), take()
    assert not names

    r, c = lax.axis_index("row"), lax.axis_index("col")
    y, x = r // NX, lax.rem(r, NX)
    z, k = c // 2, lax.rem(c, 2)
    mate = 1 - k

    def at_x(i):
        return {"row": y * NX + i}

    def at_y(i):
        return {"row": i * NX + x}

    def at_z(i):
        return {"col": i * 2 + k}

    def at_c(i):
        return {"col": i}

    partner = {"col": z * 2 + mate}

    loads = []

    def load(src, dst):
        copy = pltpu.make_async_copy(src, dst, local.at[len(loads)])
        copy.start()
        loads.append(copy)
        return copy

    barrier = pltpu.get_barrier_semaphore()

    @pl.loop(1, NX)
    def _(i):
        pl.semaphore_signal(barrier, inc=1, device_id=at_x(lax.rem(x + i, NX)), device_id_type=MESH)

    @pl.loop(1, NY)
    def _(i):
        pl.semaphore_signal(barrier, inc=1, device_id=at_y(lax.rem(y + i, NY)), device_id_type=MESH)

    @pl.loop(1, NC)
    def _(i):
        pl.semaphore_signal(barrier, inc=1, device_id=at_c(lax.rem(c + i, NC)), device_id_type=MESH)

    own = []
    for q in fwd:
        own.append(load(feat.at[:, pl.ds(fwd_at[q], FWD[q][0])], panel[q].at[y, x]))
    scalars = [
        load(rows_in, tile_rows),
        load(cols_in, tile_cols),
        load(count_in, tile_count),
        load(window_in, window),
    ]
    tile_load = load(tiles.at[0], tile.at[pl.ds(0, SLOTS)])
    feat_load = load(feat, featv)
    ws_load = load(w_self, wsv)
    bias_load = load(bias_in, bias)
    wn_load = load(w_neigh, wnv)
    cot_load = load(cot, cotv)
    for copy in own + scalars:
        copy.wait()

    pl.semaphore_wait(barrier, NX + NY + NC - 3)

    plan = Plan()
    links = Links(plan, send, recv)
    lo, hi = window[0, 0], window[0, 1]
    count = tile_count[0, 0]
    slot_row = [tile_rows[0, m] for m in range(SLOTS)]
    slot_col = [tile_cols[0, m] for m in range(SLOTS)]

    def slot_of(ids, want):
        found = jnp.int32(SLOTS)
        for m in range(SLOTS):
            found = jnp.where((ids[m] == want) & (m < count), m, found)
        return found

    def cut(ref, half):
        def view(*at):
            *lead, p = at
            if p is None:
                return ref.at[tuple(lead)]
            return ref.at[(*lead, pl.ds(half * p, half))]

        return view

    def far(d, size):
        d = d if d <= size // 2 else d - size
        return d, 1 if d > 0 else -1

    def straight(axis, size, me, device, src, dst):
        copies = []
        for d in sorted(range(1, size), key=lambda d: -abs(far(d, size)[0])):
            other = lax.rem(me + d, size)
            steps, way = far(d, size)
            copies.append(links.start(src(other), dst(me), device(other), (axis, way), abs(steps)))
        return copies

    top, low_rows = pl.ds(0, HALF), HALF // 2

    def gather0(q):
        def view(o, p):
            if p is None:
                return panel[q].at[o, :, top]
            return panel[q].at[o, pl.ds(XH * p, XH), top]

        mine = panel[q].at[y, x, top]
        copies = straight("x", NX, x, at_x, lambda o: mine, lambda i: mine)
        yield max(when for _, when in copies)
        for copy, _ in copies:
            copy.wait_recv()
        for way in (1, -1):
            plan.spawn(gather_chain(links, "y", way, NY, y, view, at_y, ready_a[q].done), plan.now)

    def gather1(q):
        deep = NY // 2

        def view(o, p):
            if p is None:
                return panel[q].at[:, o, pl.ds(HALF, HALF)]
            return panel[q].at[pl.ds(deep * p, deep), o, pl.ds(HALF, HALF)]

        def cols_then():
            for way in (1, -1):
                plan.spawn(gather_chain(links, "x", way, NX, x, view, at_x, ready_a[q].done), plan.now)

        def inner(o, p):
            if p is None:
                return panel[q].at[o, x, pl.ds(HALF, HALF)]
            return panel[q].at[o, x, pl.ds(HALF + low_rows * p, low_rows)]

        mid = Join(2, cols_then)
        for way in (1, -1):
            plan.spawn(gather_chain(links, "y", way, NY, y, inner, at_y, mid.done), plan.now)

    def gather(q):
        yield STAGGER * q
        plan.spawn(gather0(q), plan.now)
        gather1(q)

    def take_tiles():
        tile_load.wait()
        tile[SLOTS] = jnp.zeros((EDGE, EDGE), BF)
        turned[SLOTS] = jnp.zeros((EDGE, EDGE), BF)
        for q in fwd:
            prod[q][SLOTS] = jnp.zeros((EDGE, FWD[q][0]), BF)
        for q in bwd:
            back_prod[q][SLOTS] = jnp.zeros((EDGE, BWD[q][0]), BF)

    def turn(m):
        turned[m] = tile[m].T

    def degrees():
        lane = lax.broadcasted_iota(jnp.int32, (8, EDGE), 1)

        @pl.loop(0, NZ)
        def _(t):
            total = nn(jnp.ones((8, EDGE), BF), turned[slot_of(slot_row, t)])
            at = lane + t * EDGE
            total = jnp.where((at >= lo) & (at < hi), total, 0.0)
            deg_own[2 * t] = total[:, :ROWS]
            deg_own[2 * t + 1] = total[:, ROWS:]

        deg_all[c] = deg_own[c]
        degree.start()

    def self_term():
        feat_load.wait()
        ws_load.wait()
        bias_load.wait()
        pre[...] = nn(featv[...], wsv[...]) + bias[...]
        lhs[1] = featv[...]
        at = lax.broadcasted_iota(jnp.int32, (ROWS, LANES), 0) + c * ROWS
        own_in[...] = jnp.where((at >= lo) & (at < hi), 1.0, 0.0)

    def invert():
        yield 18.0
        degree.wait_recv()
        total = deg_all[0]
        for i in range(1, NC):
            total = total + deg_all[i]
        inverse = 1.0 / (1.0 + total)
        inv[...] = jnp.tile(inverse, (ROWS // 8, 1)).T
        wn_load.wait()
        cot_load.wait()
        plan.now += 0.5

    degree = Direct(links, NC, c, at_c, lambda o: deg_own.at[o], lambda i: deg_all.at[i])

    def forward(q):
        wide, direct = FWD[q]
        yield plan.now
        plan.flush()

        @pl.loop(0, SLOTS)
        def _(m):
            j = tile_cols[0, m]
            yy, xx = j // XH, lax.rem(j, XH) * 2
            prod[q][m] = nn(tile[m], panel[q][yy, pl.ds(xx, 2)].reshape(EDGE, wide)).astype(BF)

        end = Join(2, ready_b.done)
        swaps = {}
        order = [NZ // 2]
        for d in range(NZ // 2 - 1, 0, -1):
            order += [d, -d]
        order.append(0)
        for d in order:
            t = lax.rem(z + d + NZ, NZ)
            out = prod[q][slot_of(slot_row, t)]
            at = lax.broadcasted_iota(jnp.int32, (EDGE, wide), 0) + t * EDGE
            out = jnp.where((at >= lo) & (at < hi), out, jnp.zeros_like(out))
            part[q][0, t] = out[:ROWS]
            part[q][1, t] = out[ROWS:]
            swaps[d] = links.start(part[q].at[mate, t], pair[q].at[t], partner, "core")
            plan.now += 0.1

        def meet(d):
            copy, when = swaps.pop(d)
            yield when
            copy.wait_recv()
            t = lax.rem(z + d + NZ, NZ)
            pair[q][t] = pair[q][t] + part[q][k, t]

        def chain(way):
            steps, held = NZ // 2, None
            half = 0 if way > 0 else 1
            slot, block = cut(zslot[q], HALF), cut(pair[q], HALF)
            for step in range(1, steps + 1):
                d = way * (steps - step + 1)
                owner = lax.rem(z + d + NZ, NZ)
                if d in swaps:
                    yield from meet(d)
                now = half if step == 1 else None
                if held is not None:
                    yield held[1]
                    held[0].wait_recv()
                    was = half if step == 2 else None
                    add_into(block(owner, was), slot(half * steps + step - 2, was))
                    plan.now += 0.2
                held = links.start(
                    block(owner, now),
                    slot(half * steps + step - 1, now),
                    at_z(lax.rem(z + way + NZ, NZ)),
                    ("z", way),
                )
            yield held[1]
            held[0].wait_recv()
            if 0 in swaps:
                yield from meet(0)
            end.done()

        def direct_chain():
            copies = []
            for d in order:
                yield from meet(d)
                if d != 0:
                    way = 1 if d > 0 else -1
                    t = lax.rem(z + d + NZ, NZ)
                    copies.append(links.start(pair[q].at[t], zslot[q].at[z], at_z(t), ("z", way), abs(d)))
            yield max(when for _, when in copies)
            for copy, _ in copies:
                copy.wait_recv()
            ready_b.done()

        def ring():
            yield from meet(NZ // 2)
            for way in (1, -1):
                plan.spawn(chain(way), plan.now)

        if direct:
            plan.spawn(direct_chain(), plan.now)
        else:
            plan.spawn(ring(), plan.now)

    def middle():
        yield plan.now
        half = NZ // 2
        for q in fwd:
            wide, direct = FWD[q]
            total = pair[q][z].astype(F32)
            if direct:
                for d in range(1, NZ):
                    total = total + zslot[q][lax.rem(z + d, NZ)].astype(F32)
            else:
                total = total + zslot[q][half - 1].astype(F32) + zslot[q][2 * half - 1].astype(F32)
            low = (total * jnp.tile(inv[...], (1, wide // LANES))).astype(BF)
            cols = slice(fwd_at[q], fwd_at[q] + wide)
            lhs[0, :, cols] = low
            pre[...] += nn(low, wnv[cols, :])
        value = pre[...]
        s = jax.nn.sigmoid(value)
        dpre = cotv[...].astype(F32) * (s * (1.0 + value * (1.0 - s)))
        low = dpre.astype(BF)
        dlow[...] = low
        scale = inv[...] * own_in[...]
        plan.now += 1.5
        for q in bwd:
            wide = BWD[q][0]
            out = nt(low, wnv[bwd_at[q] : bwd_at[q] + wide, :]) * jnp.tile(scale, (1, wide // LANES))
            back[q][z, k] = out.astype(BF)
            plan.now += 0.4
            spread(q)
        total = jnp.sum(dpre, axis=0, keepdims=True)
        lanes = [total[:, i * LANES : (i + 1) * LANES] for i in range(WIDTH // LANES)]
        dbias[...] = jnp.concatenate(lanes + [jnp.zeros((8 - len(lanes), LANES), F32)], axis=0)
        hid[...] = (value * s).astype(BF)
        hidden_store.start()
        plan.now += 0.4
        plan.spawn(gradients(), plan.now)

        def self_back():
            selfg[...] = nt(dlow[...], wsv[...])

        plan.later(0.7, self_back)

    hidden_store = pltpu.make_async_copy(hid, hidden_out, local.at[15])

    def spread(q):
        mates = []
        view = cut(back[q], HALF)

        def pass_on(ref):
            mates.append(links.start(ref, ref, partner, "core"))

        def then():
            plan.spawn(backward(q, mates), max(when for _, when in mates))

        def direct_chain():
            mine = back[q].at[z, k]
            pass_on(mine)
            copies = []
            for d in sorted(range(1, NZ), key=lambda d: -abs(far(d, NZ)[0])):
                other = lax.rem(z + d, NZ)
                steps, way = far(d, NZ)
                copies.append((d, *links.start(mine, mine, at_z(other), ("z", way), abs(steps))))
            for d, copy, when in sorted(copies, key=lambda item: item[2]):
                yield when
                copy.wait_recv()
                pass_on(back[q].at[lax.rem(z - d + NZ, NZ), k])
            then()

        if BWD[q][1]:
            plan.spawn(direct_chain(), plan.now)
            return
        end = Join(2, then)
        for way in (1, -1):
            chain = gather_chain(
                links, "z", way, NZ, z, lambda o, p: view(o, k, p), at_z, end.done, pass_on
            )
            plan.spawn(chain, plan.now)

    def backward(q, mates):
        yield plan.now
        plan.flush()
        for copy, _ in mates:
            copy.wait_recv()
        wide = BWD[q][0]

        @pl.loop(0, SLOTS)
        def _(m):
            t = tile_rows[0, m]
            back_prod[q][m] = nn(turned[m], back[q][t].reshape(EDGE, wide)).astype(BF)

        @pl.loop(0, NY * XH)
        def _(j):
            out = back_prod[q][slot_of(slot_col, j)]
            yy, xx = j // XH, lax.rem(j, XH) * 2
            for i in range(2):
                colp[q][yy, xx + i] = out[i * ROWS : (i + 1) * ROWS]

        plan.now += 2.0
        scatter0(q)
        scatter1(q)

    def scatter0(q):
        last_y = NY // 2 - 1

        def tail():
            copies = straight("x", NX, x, at_x, lambda o: colp[q].at[y, o, top], lambda i: rx0[q].at[i])
            yield max(when for _, when in copies)
            for copy, _ in copies:
                copy.wait_recv()
            write(q, 0, [rx0[q][lax.rem(x + d, NX)] for d in range(1, NX)])

        def then():
            for w in range(2):
                add_into(colp[q].at[y, :, top], ry0[q].at[w, last_y])
            plan.spawn(tail(), plan.now)

        def block(o, p):
            if p is None:
                return colp[q].at[o, :, top]
            return colp[q].at[o, pl.ds(XH * p, XH), top]

        mid = Join(2, then)
        slot = cut(ry0[q], XH)
        for w, way in enumerate((1, -1)):
            chain = scatter_chain(
                links, "y", way, NY, y, block, lambda step, p, w=w: slot(w, step - 1, p), at_y, mid.done
            )
            plan.spawn(chain, plan.now)

    def scatter1(q):
        last_y, last_x = NY // 2 - 1, NX // 2 - 1
        deep = NY // 2
        bottom = pl.ds(HALF, HALF)

        def finish():
            write(q, 1, [ry1[q][last_y], ry1[q][NY - 1]])

        def inner(o, p):
            if p is None:
                return colp[q].at[o, x, bottom]
            return colp[q].at[o, x, pl.ds(HALF + low_rows * p, low_rows)]

        def then():
            for w in range(2):
                add_into(colp[q].at[:, x, bottom], rx1[q].at[w, last_x])
            end = Join(2, finish)
            slot = cut(ry1[q], low_rows)
            for w, way in enumerate((1, -1)):
                chain = scatter_chain(
                    links,
                    "y",
                    way,
                    NY,
                    y,
                    inner,
                    lambda step, p, w=w: slot(w * (NY // 2) + step - 1, p),
                    at_y,
                    end.done,
                )
                plan.spawn(chain, plan.now)

        def block(o, p):
            if p is None:
                return colp[q].at[:, o, bottom]
            return colp[q].at[pl.ds(deep * p, deep), o, bottom]

        mid = Join(2, then)
        slot = cut(rx1[q], deep)
        for w, way in enumerate((1, -1)):
            chain = scatter_chain(
                links, "x", way, NX, x, block, lambda step, p, w=w: slot(w, step - 1, p), at_x, mid.done
            )
            plan.spawn(chain, plan.now)

    def write(q, h, terms):
        rows, cols = slice(HALF * h, HALF * (h + 1)), slice(bwd_at[q], bwd_at[q] + BWD[q][0])
        total = colp[q][y, x, rows].astype(F32)
        for term in terms:
            total = total + term.astype(F32)
        gft[rows, cols] = (total + selfg[rows, cols]).astype(BF)

    def gradients():
        swaps = [
            links.start(lhs.at[mate], lhs_in, partner, "core"),
            links.start(dlow, dlow_in, partner, "core"),
            links.start(dbias, dbias_in, partner, "core"),
        ]
        yield swaps[-1][1]
        for copy, _ in swaps:
            copy.wait_recv()
        bz_in[z] = dbias[...] + dbias_in[...]
        bias_z.start()
        yield plan.now
        wide = WIDTH // 4
        for i in range(4):
            at = slice(i * wide, (i + 1) * wide)
            left = jnp.concatenate([lhs[k, :, at], lhs_in[:, at]], axis=0)
            both = jnp.concatenate([dlow[...], dlow_in[...]], axis=0)
            out = nn(left.T, both)
            for j in range(wide // DEEP):
                ez[i * (wide // DEEP) + j] = out[j * DEEP : (j + 1) * DEEP].astype(BF)
            plan.now += 0.4
            yield plan.now
        end = Join(2, lambda: plan.spawn(plane_sum(), plan.now))
        block, slot = cut(ez, DEEP // 2), cut(ez_in, DEEP // 2)
        for w, way in enumerate((1, -1)):
            plan.spawn(
                scatter_chain(
                    links,
                    "z",
                    way,
                    NZ,
                    z,
                    block,
                    lambda step, p, w=w: slot(w, step - 1, p),
                    at_z,
                    end.done,
                ),
                plan.now,
            )

    def plane_sum():
        yield plan.now
        bias_z.wait_recv()
        last = NZ // 2 - 1
        total = ez[z].astype(F32) + ez_in[0, last].astype(F32) + ez_in[1, last].astype(F32)
        low = bz_in[0]
        for i in range(1, NZ):
            low = low + bz_in[i]
        for j in range(NX):
            ex[j, 0:DEEP] = total[:, j * LANES : (j + 1) * LANES]
            ex[j, DEEP : DEEP + 8] = low
        ex_in[x] = ex[x]
        sum_x.start()
        yield plan.now + PLANE
        sum_x.wait_recv()
        total = ex_in[0]
        for i in range(1, NX):
            total = total + ex_in[i]
        for i in range(NY):
            ey[i, 0:8] = total[8 * i : 8 * i + 8]
            ey[i, 8:16] = total[DEEP : DEEP + 8]
        ey_in[y] = ey[y]
        sum_y.start()
        yield plan.now + PLANE
        sum_y.wait_recv()
        total = ey_in[0]
        for i in range(1, NY):
            total = total + ey_in[i]
        total = total * factor
        ag[y] = total[0:8]
        all_y.start()
        for j in range(WIDTH // LANES):
            gb[:, j * LANES : (j + 1) * LANES] = total[8 + j : 9 + j]
        yield plan.now + PLANE
        all_y.wait_recv()
        low = jnp.concatenate([ag[i] for i in range(NY)], axis=0).astype(BF)
        grads[k, z, :, lanes_of(x)] = low
        all_x.start()
        yield plan.now + PLANE
        all_x.wait_recv()
        mates = []
        end = Join(2, lambda: plan.spawn(collect(mates), max(when for _, when in mates)))
        view = cut(grads, DEEP // 2)
        for way in (1, -1):
            chain = gather_chain(
                links,
                "z",
                way,
                NZ,
                z,
                lambda o, p: view(k, o, p),
                at_z,
                end.done,
                lambda ref: mates.append(links.start(ref, ref, partner, "core")),
            )
            plan.spawn(chain, plan.now)

    def collect(mates):
        yield plan.now
        for copy, _ in mates:
            copy.wait_recv()

    factor = 1.0 / math.sqrt(ROWS * NR * NC)
    bias_z = Direct(links, NZ, z, at_z, lambda o: bz_in.at[z], lambda i: bz_in.at[i])
    sum_x = Direct(links, NX, x, at_x, lambda o: ex.at[o], lambda i: ex_in.at[i])
    sum_y = Direct(links, NY, y, at_y, lambda o: ey.at[o], lambda i: ey_in.at[i])
    all_y = Direct(links, NY, y, at_y, lambda o: ag.at[y], lambda i: ag.at[i])

    def lanes_of(i):
        return pl.ds(pl.multiple_of(i * LANES, LANES), LANES)

    all_x = Direct(
        links,
        NX,
        x,
        at_x,
        lambda o: grads.at[k, z, :, lanes_of(x)],
        lambda i: grads.at[k, z, :, lanes_of(i)],
    )

    ready_a = [Join(4, lambda q=q: plan.spawn(forward(q), plan.now)) for q in fwd]
    ready_b = Join(len(FWD), lambda: plan.spawn(middle(), plan.now))
    for q in fwd:
        plan.spawn(gather(q), STAGGER * q)
    plan.later(0.4, take_tiles)
    for m in range(SLOTS):
        plan.later(0.3, functools.partial(turn, m))
    plan.later(1.5, degrees)
    plan.later(1.0, self_term)
    plan.spawn(invert(), 10.0)
    plan.run()
    assert links.used <= SEMS

    stores = [
        pltpu.make_async_copy(gft, gfeat_out, local.at[16]),
        pltpu.make_async_copy(grads, grads_out, local.at[17]),
        pltpu.make_async_copy(gb, gbias_out, local.at[18]),
    ]
    for copy in stores:
        copy.start()
    links.finish()
    hidden_store.wait()
    for copy in stores:
        copy.wait()


def write_out(hidden, gfeat, grads, gbias, hidden_out, gfeat_out, gneigh_out, gself_out, gbias_out, *scratch):
    *held, sems = scratch
    sources = [grads.at[0], grads.at[1], hidden, gfeat, gbias]
    targets = [gneigh_out, gself_out, hidden_out, gfeat_out, gbias_out]
    count = len(held)
    takes = [pltpu.make_async_copy(a, b, sems.at[i]) for i, (a, b) in enumerate(zip(sources, held))]
    gives = [pltpu.make_async_copy(a, b, sems.at[count + i]) for i, (a, b) in enumerate(zip(held, targets))]
    for copy in takes:
        copy.start()
    for take, give in zip(takes, gives):
        take.wait()
        give.start()
    for copy in gives:
        copy.wait()


def on_device(
    features, tile_vals, tile_rows, tile_cols, tile_count, window, w_neigh, w_self, layer_bias, cotangent
):
    rows, width = features.shape
    slots, edge = tile_vals.shape[1:3]
    ny = lax.axis_size("row") // NX
    nz = lax.axis_size("col") // 2
    nc = 2 * nz

    def vmem(*shape, dtype=BF):
        return pltpu.VMEM(shape, dtype)

    fwd, bwd = [w for w, _ in FWD], [w for w, _ in BWD]
    each = [
        (fwd, (ny, NX, ROWS)),
        (fwd, (2, nz, ROWS)),
        (fwd, (nz, ROWS)),
        (fwd, (nz, ROWS)),
        (fwd, (slots + 1, edge)),
        (bwd, (nz, 2, ROWS)),
        (bwd, (slots + 1, edge)),
        (bwd, (ny, NX, ROWS)),
        (bwd, (2, ny // 2, NX, HALF)),
        (bwd, (NX, HALF)),
        (bwd, (2, NX // 2, ny, HALF)),
        (bwd, (ny, HALF)),
    ]
    deep = width // nz
    scratch = [vmem(*shape, w) for widths, shape in each for w in widths]
    scratch += [vmem(slots + 1, edge, edge)] * 2
    scratch += [vmem(rows, width), vmem(rows, width), vmem(width, width), vmem(width, width)]
    scratch += [vmem(1, width, dtype=F32)]
    scratch += [vmem(nc, 8, ROWS, dtype=F32)] * 2
    scratch += [vmem(ROWS, LANES, dtype=F32)] * 2
    scratch += [vmem(rows, width, dtype=F32)] * 2
    scratch += [vmem(2, rows, width), vmem(rows, width)]
    scratch += [vmem(rows, width)] * 2
    scratch += [vmem(8, LANES, dtype=F32)] * 2
    scratch += [vmem(nz, deep, width), vmem(2, nz // 2, deep, width)]
    scratch += [vmem(nz, 8, LANES, dtype=F32)]
    scratch += [vmem(NX, deep + 8, LANES, dtype=F32)] * 2
    scratch += [vmem(ny, 16, LANES, dtype=F32)] * 2
    scratch += [vmem(ny, 8, LANES, dtype=F32)]
    scratch += [vmem(2, nz, deep, width)]
    scratch += [vmem(rows, width)] * 2 + [vmem(1, width, dtype=F32)]
    scratch += [pltpu.SMEM(a.shape, jnp.int32) for a in (tile_rows, tile_cols, tile_count, window)]
    scratch += [pltpu.SemaphoreType.DMA((SEMS,))] * 2 + [pltpu.SemaphoreType.DMA((20,))]
    anywhere = pl.BlockSpec(memory_space=pl.ANY)
    far = pl.BlockSpec(memory_space=pltpu.HBM)
    sizes = (ny, nz, slots, edge, width)
    matrix = jax.ShapeDtypeStruct((rows, width), BF)
    weight = jax.ShapeDtypeStruct((nz, deep, width), BF)
    vector = jax.ShapeDtypeStruct((1, width), F32)
    results = pl.pallas_call(
        functools.partial(layer, sizes),
        out_shape=(matrix, matrix, jax.ShapeDtypeStruct((2, nz, deep, width), BF), vector),
        in_specs=[far] * 10,
        out_specs=(anywhere,) * 4,
        scratch_shapes=scratch,
        compiler_params=pltpu.CompilerParams(
            collective_id=0, has_side_effects=True, vmem_limit_bytes=VMEM_LIMIT
        ),
    )(
        features,
        tile_vals,
        tile_rows,
        tile_cols,
        tile_count,
        window,
        w_neigh,
        w_self,
        layer_bias.reshape(1, width),
        cotangent,
    )
    hidden, gfeat, gneigh, gself, gbias = pl.pallas_call(
        write_out,
        out_shape=(matrix, matrix, weight, weight, vector),
        in_specs=[anywhere] * 4,
        out_specs=(far,) * 5,
        scratch_shapes=[
            vmem(nz, deep, width),
            vmem(nz, deep, width),
            vmem(rows, width),
            vmem(rows, width),
            vmem(1, width, dtype=F32),
            pltpu.SemaphoreType.DMA((10,)),
        ],
        compiler_params=pltpu.CompilerParams(vmem_limit_bytes=VMEM_LIMIT),
    )(*results)
    return hidden, gfeat, gneigh.reshape(width, width), gself.reshape(width, width), gbias.reshape(width)


def solution(mesh):
    in_specs = (
        P(("col", "row"), None),
        P("row", "col", None, None),
        P("row", "col"),
        P("row", "col"),
        P("row", "col"),
        P("row", None),
        P(),
        P(),
        P(),
        P(("col", "row"), None),
    )
    out_specs = (P(("col", "row"), None), P(("col", "row"), None), P(), P(), P())
    return jax.shard_map(
        on_device, mesh=mesh, in_specs=in_specs, out_specs=out_specs, check_vma=False
    )
```

```python
import functools
import heapq
import math

import jax
import jax.numpy as jnp
from jax import lax
from jax.experimental import pallas as pl
from jax.experimental.pallas import tpu as pltpu
from jax.sharding import PartitionSpec as P

MESH = pl.DeviceIdType.MESH
BF = jnp.bfloat16
F32 = jnp.float32

NX = 4
FWD = ((256, False), (256, False),)
BWD = ((256, False), (256, False),)
STAGGER = 0
TOP_FWD, TOP_BWD = 48, 64
ROWS = 128
HALF = ROWS // 2
LANES = 128
SEMS = 480
VMEM_LIMIT = 63 * 1024 * 1024
LINK_RATE, HOP = 88e3, 2.3
CORE_RATE, CORE_HOP = 350e3, 0.9
ISSUE = 0.07
PLANE = 3.5


def nn(a, b):
    return jnp.dot(a, b, preferred_element_type=F32)


def nt(a, b):
    return lax.dot_general(a, b, (((1,), (1,)), ((), ())), preferred_element_type=F32)


class Plan:
    def __init__(self):
        self.heap, self.count, self.now, self.idle = [], 0, 0.0, []

    def spawn(self, chain, when):
        heapq.heappush(self.heap, (when, self.count, chain))
        self.count += 1

    def later(self, cost, work):
        self.idle.append((cost, work))

    def flush(self):
        while self.idle:
            cost, work = self.idle.pop(0)
            work()
            self.now += cost

    def run(self):
        while self.heap or self.idle:
            if self.idle and (not self.heap or self.heap[0][0] > self.now + self.idle[0][0]):
                cost, work = self.idle.pop(0)
                work()
                self.now += cost
                continue
            when, _, chain = heapq.heappop(self.heap)
            self.now = max(self.now, when)
            try:
                self.spawn(chain, next(chain))
            except StopIteration:
                pass


class Join:
    def __init__(self, count, then):
        self.count, self.then = count, then

    def done(self):
        self.count -= 1
        if self.count == 0:
            self.then()


class Links:
    def __init__(self, plan, send, recv):
        self.plan, self.send, self.recv, self.used, self.sent = plan, send, recv, 0, []
        self.free = {}

    def start(self, src, dst, device, link, hops=1):
        at = self.used
        self.used += 1
        copy = pltpu.make_async_remote_copy(
            src_ref=src,
            dst_ref=dst,
            send_sem=self.send.at[at],
            recv_sem=self.recv.at[at],
            device_id=device,
            device_id_type=MESH,
        )
        copy.start()
        self.sent.append(copy)
        size = math.prod(src.shape) * src.dtype.itemsize
        rate, hop = (CORE_RATE, CORE_HOP) if link == "core" else (LINK_RATE / 2, HOP)
        self.plan.now += ISSUE
        ready = max(self.plan.now, self.free.get(link, 0.0)) + hops * size / rate
        self.free[link] = ready
        return copy, ready + hop + 0.3 * (hops - 1)

    def finish(self):
        for copy in self.sent:
            copy.wait_send()


class Direct:
    def __init__(self, links, size, me, device, src, dst):
        self.links, self.size, self.me = links, size, me
        self.device, self.src, self.dst = device, src, dst
        self.base = links.used
        links.used += size - 1
        links.sent.append(self)

    def copy(self, step):
        other = lax.rem(self.me + step, self.size)
        return pltpu.make_async_remote_copy(
            src_ref=self.src(other),
            dst_ref=self.dst(self.me),
            send_sem=self.links.send.at[self.base + step - 1],
            recv_sem=self.links.recv.at[self.base + step - 1],
            device_id=self.device(other),
            device_id_type=MESH,
        )

    def start(self):
        @pl.loop(1, self.size)
        def _(step):
            self.copy(step).start()

        self.links.plan.now += ISSUE * self.size

    def wait_recv(self):
        @pl.loop(1, self.size)
        def _(step):
            self.copy(step).wait_recv()

    def wait_send(self):
        @pl.loop(1, self.size)
        def _(step):
            self.copy(step).wait_send()


def gather_chain(links, axis, way, size, me, block, device, done, pass_on=None):
    steps, held = size // 2, None
    half = 0 if way > 0 else 1
    for step in range(1, steps + 2):
        owner = lax.rem(me - way * (step - 1) + size, size)
        if held is not None:
            yield held[1]
            held[0].wait_recv()
        if step <= steps:
            ref = block(owner, None if step < steps else half)
            held = links.start(ref, ref, device(lax.rem(me + way + size, size)), (axis, way))
        if pass_on is not None and (step > 1 or way > 0):
            pass_on(owner, None if step <= steps else half)
    done()


def scatter_chain(links, axis, way, size, me, block, slot, device, done):
    steps, held = size // 2, None
    half = 0 if way > 0 else 1
    for step in range(1, steps + 1):
        owner = lax.rem(me + way * (steps - step + 1) + size, size)
        part = half if step == 1 else None
        if held is not None:
            yield held[1]
            held[0].wait_recv()
            was = half if step == 2 else None
            add_into(block(owner, was), slot(step - 1, was))
            links.plan.now += 0.2
        held = links.start(
            block(owner, part), slot(step, part), device(lax.rem(me + way + size, size)), (axis, way)
        )
    yield held[1]
    held[0].wait_recv()
    done()


def add_into(to, frm):
    to[...] = to[...] + frm[...]


def layer(
    sizes,
    feat,
    tiles,
    rows_in,
    cols_in,
    count_in,
    window_in,
    w_neigh,
    w_self,
    bias_in,
    cot,
    hidden_out,
    gfeat_out,
    grads_out,
    gbias_out,
    *scratch,
):
    names = list(scratch)

    def take():
        return names.pop(0)

    NY, NZ, SLOTS, EDGE, WIDTH = sizes
    NC, NR = 2 * NZ, NX * NY
    XH = NX // 2
    DEEP = WIDTH // NZ
    fwd, bwd = range(len(FWD)), range(len(BWD))
    fwd_at = [sum(w for w, _ in FWD[:q]) for q in fwd]
    bwd_at = [sum(w for w, _ in BWD[:q]) for q in bwd]
    panel = [take() for _ in fwd]
    part = [take() for _ in fwd]
    pair = [take() for _ in fwd]
    zslot = [take() for _ in fwd]
    prod = [take() for _ in fwd]
    back = [take() for _ in bwd]
    back_prod = [take() for _ in bwd]
    colp = [take() for _ in bwd]
    ry0 = [take() for _ in bwd]
    rx0 = [take() for _ in bwd]
    rx1 = [take() for _ in bwd]
    ry1 = [take() for _ in bwd]
    tile = take()
    turned = take()
    featv, cotv, wnv, wsv = take(), take(), take(), take()
    bias = take()
    deg_own, deg_all = take(), take()
    own_in, inv = take(), take()
    pre = take()
    selfg = take()
    lhs, lhs_in = take(), take()
    dlow, dlow_in = take(), take()
    dbias, dbias_in = take(), take()
    ez, ez_in = take(), take()
    bz_in = take()
    ex, ex_in = take(), take()
    ey, ey_in = take(), take()
    ag = take()
    grads = take()
    hid, gft, gb = take(), take(), take()
    tile_rows, tile_cols, tile_count, window = take(), take(), take(), take()
    send, recv, local = take(), take(), take()
    assert not names

    r, c = lax.axis_index("row"), lax.axis_index("col")
    y, x = r // NX, lax.rem(r, NX)
    z, k = c // 2, lax.rem(c, 2)
    mate = 1 - k

    def at_x(i):
        return {"row": y * NX + i}

    def at_y(i):
        return {"row": i * NX + x}

    def at_z(i):
        return {"col": i * 2 + k}

    def at_c(i):
        return {"col": i}

    partner = {"col": z * 2 + mate}

    loads = []

    def load(src, dst):
        copy = pltpu.make_async_copy(src, dst, local.at[len(loads)])
        copy.start()
        loads.append(copy)
        return copy

    barrier = pltpu.get_barrier_semaphore()

    @pl.loop(1, NX)
    def _(i):
        pl.semaphore_signal(barrier, inc=1, device_id=at_x(lax.rem(x + i, NX)), device_id_type=MESH)

    @pl.loop(1, NY)
    def _(i):
        pl.semaphore_signal(barrier, inc=1, device_id=at_y(lax.rem(y + i, NY)), device_id_type=MESH)

    @pl.loop(1, NC)
    def _(i):
        pl.semaphore_signal(barrier, inc=1, device_id=at_c(lax.rem(c + i, NC)), device_id_type=MESH)

    own = []
    for q in fwd:
        own.append(load(feat.at[:, pl.ds(fwd_at[q], FWD[q][0])], panel[q].at[y, x]))
    scalars = [
        load(rows_in, tile_rows),
        load(cols_in, tile_cols),
        load(count_in, tile_count),
        load(window_in, window),
    ]
    tile_load = load(tiles.at[0], tile.at[pl.ds(0, SLOTS)])
    feat_load = load(feat, featv)
    ws_load = load(w_self, wsv)
    bias_load = load(bias_in, bias)
    wn_load = load(w_neigh, wnv)
    cot_load = load(cot, cotv)
    for copy in own + scalars:
        copy.wait()

    pl.semaphore_wait(barrier, NX + NY + NC - 3)

    plan = Plan()
    links = Links(plan, send, recv)
    lo, hi = window[0, 0], window[0, 1]
    count = tile_count[0, 0]
    slot_row = [tile_rows[0, m] for m in range(SLOTS)]
    slot_col = [tile_cols[0, m] for m in range(SLOTS)]

    def slot_of(ids, want):
        found = jnp.int32(SLOTS)
        for m in range(SLOTS):
            found = jnp.where((ids[m] == want) & (m < count), m, found)
        return found

    def cut(ref, half):
        def view(*at):
            *lead, p = at
            if p is None:
                return ref.at[tuple(lead)]
            return ref.at[(*lead, pl.ds(half * p, half))]

        return view

    def far(d, size):
        d = d if d <= size // 2 else d - size
        return d, 1 if d > 0 else -1

    def straight(axis, size, me, device, src, dst):
        copies = []
        for d in sorted(range(1, size), key=lambda d: -abs(far(d, size)[0])):
            other = lax.rem(me + d, size)
            steps, way = far(d, size)
            copies.append(links.start(src(other), dst(me), device(other), (axis, way), abs(steps)))
        return copies

    def lanes_half(ref, at, p, wide):
        if p is None:
            return ref.at[at]
        return ref.at[(*at, pl.ds(p * (wide // 2), wide // 2))]

    def gather0(q):
        rows, wide = pl.ds(0, TOP_FWD), FWD[q][0]

        def along_y(b):
            for way in (1, -1):
                chain = gather_chain(
                    links,
                    "y",
                    way,
                    NY,
                    y,
                    lambda o, p: lanes_half(panel[q], (o, b, rows), p, wide),
                    at_y,
                    ready_a[q].done,
                )
                plan.spawn(chain, plan.now)

        halves = []

        def arrived(b, p):
            if p is not None:
                halves.append(b)
                if len(halves) < 2:
                    return
            along_y(b)

        for way in (1, -1):
            chain = gather_chain(
                links,
                "x",
                way,
                NX,
                x,
                lambda o, p: lanes_half(panel[q], (y, o, rows), p, wide),
                at_x,
                lambda: None,
                arrived,
            )
            plan.spawn(chain, plan.now)

    def gather1(q):
        rows, wide = pl.ds(TOP_FWD, ROWS - TOP_FWD), FWD[q][0]
        halves = []

        def along_x(b):
            for way in (1, -1):
                chain = gather_chain(
                    links,
                    "x",
                    way,
                    NX,
                    x,
                    lambda o, p: lanes_half(panel[q], (b, o, rows), p, wide),
                    at_x,
                    ready_a[q].done,
                )
                plan.spawn(chain, plan.now)

        def arrived(b, p):
            if p is not None:
                halves.append(b)
                if len(halves) < 2:
                    return
            along_x(b)

        for way in (1, -1):
            chain = gather_chain(
                links,
                "y",
                way,
                NY,
                y,
                lambda o, p: lanes_half(panel[q], (o, x, rows), p, wide),
                at_y,
                lambda: None,
                arrived,
            )
            plan.spawn(chain, plan.now)

    def gather(q):
        yield STAGGER * q
        gather0(q)
        gather1(q)

    def take_tiles():
        tile_load.wait()
        tile[SLOTS] = jnp.zeros((EDGE, EDGE), BF)
        turned[SLOTS] = jnp.zeros((EDGE, EDGE), BF)
        for q in fwd:
            prod[q][SLOTS] = jnp.zeros((EDGE, FWD[q][0]), BF)
        for q in bwd:
            back_prod[q][SLOTS] = jnp.zeros((EDGE, BWD[q][0]), BF)

    def turn(m):
        turned[m] = tile[m].T

    def degrees():
        lane = lax.broadcasted_iota(jnp.int32, (8, EDGE), 1)

        @pl.loop(0, NZ)
        def _(t):
            total = nn(jnp.ones((8, EDGE), BF), turned[slot_of(slot_row, t)])
            at = lane + t * EDGE
            total = jnp.where((at >= lo) & (at < hi), total, 0.0)
            deg_own[2 * t] = total[:, :ROWS]
            deg_own[2 * t + 1] = total[:, ROWS:]

        deg_all[c] = deg_own[c]
        degree.start()

    def self_term():
        feat_load.wait()
        ws_load.wait()
        bias_load.wait()
        pre[...] = nn(featv[...], wsv[...]) + bias[...]
        lhs[1] = featv[...]
        at = lax.broadcasted_iota(jnp.int32, (ROWS, LANES), 0) + c * ROWS
        own_in[...] = jnp.where((at >= lo) & (at < hi), 1.0, 0.0)

    def invert():
        yield 6.0
        plan.flush()
        yield 18.0
        degree.wait_recv()
        total = deg_all[0]
        for i in range(1, NC):
            total = total + deg_all[i]
        inverse = 1.0 / (1.0 + total)
        inv[...] = jnp.tile(inverse, (ROWS // 8, 1)).T
        wn_load.wait()
        cot_load.wait()
        plan.now += 0.5

    degree = Direct(links, NC, c, at_c, lambda o: deg_own.at[o], lambda i: deg_all.at[i])

    def forward(q):
        wide, direct = FWD[q]
        yield plan.now
        plan.flush()

        @pl.loop(0, SLOTS)
        def _(m):
            j = tile_cols[0, m]
            yy, xx = j // XH, lax.rem(j, XH) * 2
            prod[q][m] = nn(tile[m], panel[q][yy, pl.ds(xx, 2)].reshape(EDGE, wide)).astype(BF)

        end = Join(2, ready_b.done)
        swaps = {}
        order = [NZ // 2]
        for d in range(NZ // 2 - 1, 0, -1):
            order += [d, -d]
        order.append(0)
        for d in order:
            t = lax.rem(z + d + NZ, NZ)
            out = prod[q][slot_of(slot_row, t)]
            at = lax.broadcasted_iota(jnp.int32, (EDGE, wide), 0) + t * EDGE
            out = jnp.where((at >= lo) & (at < hi), out, jnp.zeros_like(out))
            part[q][0, t] = out[:ROWS]
            part[q][1, t] = out[ROWS:]
            swaps[d] = links.start(part[q].at[mate, t], pair[q].at[t], partner, "core")
            plan.now += 0.1

        def meet(d):
            copy, when = swaps.pop(d)
            yield when
            copy.wait_recv()
            t = lax.rem(z + d + NZ, NZ)
            pair[q][t] = pair[q][t] + part[q][k, t]

        def chain(way):
            steps, held = NZ // 2, None
            half = 0 if way > 0 else 1
            slot, block = cut(zslot[q], HALF), cut(pair[q], HALF)
            for step in range(1, steps + 1):
                d = way * (steps - step + 1)
                owner = lax.rem(z + d + NZ, NZ)
                if d in swaps:
                    yield from meet(d)
                now = half if step == 1 else None
                if held is not None:
                    yield held[1]
                    held[0].wait_recv()
                    was = half if step == 2 else None
                    add_into(block(owner, was), slot(half * steps + step - 2, was))
                    plan.now += 0.2
                held = links.start(
                    block(owner, now),
                    slot(half * steps + step - 1, now),
                    at_z(lax.rem(z + way + NZ, NZ)),
                    ("z", way),
                )
            yield held[1]
            held[0].wait_recv()
            if 0 in swaps:
                yield from meet(0)
            end.done()

        def direct_chain():
            copies = []
            for d in order:
                yield from meet(d)
                if d != 0:
                    way = 1 if d > 0 else -1
                    t = lax.rem(z + d + NZ, NZ)
                    copies.append(links.start(pair[q].at[t], zslot[q].at[z], at_z(t), ("z", way), abs(d)))
            yield max(when for _, when in copies)
            for copy, _ in copies:
                copy.wait_recv()
            ready_b.done()

        def ring():
            yield from meet(NZ // 2)
            for way in (1, -1):
                plan.spawn(chain(way), plan.now)

        if direct:
            plan.spawn(direct_chain(), plan.now)
        else:
            plan.spawn(ring(), plan.now)

    def middle():
        yield plan.now
        half = NZ // 2
        for q in fwd:
            wide, direct = FWD[q]
            total = pair[q][z].astype(F32)
            if direct:
                for d in range(1, NZ):
                    total = total + zslot[q][lax.rem(z + d, NZ)].astype(F32)
            else:
                total = total + zslot[q][half - 1].astype(F32) + zslot[q][2 * half - 1].astype(F32)
            low = (total * jnp.tile(inv[...], (1, wide // LANES))).astype(BF)
            cols = slice(fwd_at[q], fwd_at[q] + wide)
            lhs[0, :, cols] = low
            pre[...] += nn(low, wnv[cols, :])
        swaps = [links.start(lhs.at[mate], lhs_in, partner, "core")]
        value = pre[...]
        s = jax.nn.sigmoid(value)
        dpre = cotv[...].astype(F32) * (s * (1.0 + value * (1.0 - s)))
        low = dpre.astype(BF)
        dlow[...] = low
        swaps.append(links.start(dlow, dlow_in, partner, "core"))
        scale = inv[...] * own_in[...]
        plan.now += 1.5
        for q in bwd:
            wide = BWD[q][0]
            out = nt(low, wnv[bwd_at[q] : bwd_at[q] + wide, :]) * jnp.tile(scale, (1, wide // LANES))
            back[q][z, k] = out.astype(BF)
            plan.now += 0.4
            spread(q)
        total = jnp.sum(dpre, axis=0, keepdims=True)
        lanes = [total[:, i * LANES : (i + 1) * LANES] for i in range(WIDTH // LANES)]
        dbias[...] = jnp.concatenate(lanes + [jnp.zeros((8 - len(lanes), LANES), F32)], axis=0)
        hid[...] = (value * s).astype(BF)
        hidden_store.start()
        plan.now += 0.4
        plan.spawn(gradients(swaps), plan.now)

        def self_back():
            selfg[...] = nt(dlow[...], wsv[...])

        plan.later(0.7, self_back)

    hidden_store = pltpu.make_async_copy(hid, hidden_out, local.at[15])

    def spread(q):
        mates = []
        view = cut(back[q], HALF)

        def pass_on(o, p):
            ref = view(o, k, p)
            mates.append(links.start(ref, ref, partner, "core"))

        def then():
            plan.spawn(backward(q, mates), max(when for _, when in mates))

        def direct_chain():
            mine = back[q].at[z, k]
            pass_on(z, None)
            copies = []
            for d in sorted(range(1, NZ), key=lambda d: -abs(far(d, NZ)[0])):
                other = lax.rem(z + d, NZ)
                steps, way = far(d, NZ)
                copies.append((d, *links.start(mine, mine, at_z(other), ("z", way), abs(steps))))
            for d, copy, when in sorted(copies, key=lambda item: item[2]):
                yield when
                copy.wait_recv()
                pass_on(lax.rem(z - d + NZ, NZ), None)
            then()

        if BWD[q][1]:
            plan.spawn(direct_chain(), plan.now)
            return
        end = Join(2, then)
        for way in (1, -1):
            chain = gather_chain(
                links, "z", way, NZ, z, lambda o, p: view(o, k, p), at_z, end.done, pass_on
            )
            plan.spawn(chain, plan.now)

    def backward(q, mates):
        yield plan.now
        plan.flush()
        for copy, _ in mates:
            copy.wait_recv()
        wide = BWD[q][0]

        @pl.loop(0, SLOTS)
        def _(m):
            t = tile_rows[0, m]
            back_prod[q][m] = nn(turned[m], back[q][t].reshape(EDGE, wide)).astype(BF)

        @pl.loop(0, NY * XH)
        def _(j):
            out = back_prod[q][slot_of(slot_col, j)]
            yy, xx = j // XH, lax.rem(j, XH) * 2
            for i in range(2):
                colp[q][yy, xx + i] = out[i * ROWS : (i + 1) * ROWS]

        plan.now += 2.0
        scatter0(q)
        scatter1(q)

    top, low_rows = pl.ds(0, HALF), HALF // 2

    def scatter0(q):
        last_y = NY // 2 - 1

        def tail():
            copies = straight("x", NX, x, at_x, lambda o: colp[q].at[y, o, top], lambda i: rx0[q].at[i])
            yield max(when for _, when in copies)
            for copy, _ in copies:
                copy.wait_recv()
            write(q, 0, [rx0[q][lax.rem(x + d, NX)] for d in range(1, NX)])

        def then():
            for w in range(2):
                add_into(colp[q].at[y, :, top], ry0[q].at[w, last_y])
            plan.spawn(tail(), plan.now)

        def block(o, p):
            if p is None:
                return colp[q].at[o, :, top]
            return colp[q].at[o, pl.ds(XH * p, XH), top]

        mid = Join(2, then)
        slot = cut(ry0[q], XH)
        for w, way in enumerate((1, -1)):
            chain = scatter_chain(
                links, "y", way, NY, y, block, lambda step, p, w=w: slot(w, step - 1, p), at_y, mid.done
            )
            plan.spawn(chain, plan.now)

    def scatter1(q):
        last_y, last_x = NY // 2 - 1, NX // 2 - 1
        deep = NY // 2
        bottom = pl.ds(HALF, HALF)

        def finish():
            write(q, 1, [ry1[q][last_y], ry1[q][NY - 1]])

        def inner(o, p):
            if p is None:
                return colp[q].at[o, x, bottom]
            return colp[q].at[o, x, pl.ds(HALF + low_rows * p, low_rows)]

        def then():
            for w in range(2):
                add_into(colp[q].at[:, x, bottom], rx1[q].at[w, last_x])
            end = Join(2, finish)
            slot = cut(ry1[q], low_rows)
            for w, way in enumerate((1, -1)):
                chain = scatter_chain(
                    links,
                    "y",
                    way,
                    NY,
                    y,
                    inner,
                    lambda step, p, w=w: slot(w * (NY // 2) + step - 1, p),
                    at_y,
                    end.done,
                )
                plan.spawn(chain, plan.now)

        def block(o, p):
            if p is None:
                return colp[q].at[:, o, bottom]
            return colp[q].at[pl.ds(deep * p, deep), o, bottom]

        mid = Join(2, then)
        slot = cut(rx1[q], deep)
        for w, way in enumerate((1, -1)):
            chain = scatter_chain(
                links, "x", way, NX, x, block, lambda step, p, w=w: slot(w, step - 1, p), at_x, mid.done
            )
            plan.spawn(chain, plan.now)

    def write(q, h, terms):
        rows = slice(TOP_BWD, ROWS) if h else slice(0, TOP_BWD)
        cols = slice(bwd_at[q], bwd_at[q] + BWD[q][0])
        total = colp[q][y, x, rows].astype(F32)
        for term in terms:
            total = total + term.astype(F32)
        gft[rows, cols] = (total + selfg[rows, cols]).astype(BF)

    def gradients(swaps):
        meet, when = links.start(dbias, dbias_in, partner, "core")
        yield swaps[-1][1]
        for copy, _ in swaps:
            copy.wait_recv()
        wide = WIDTH // 4
        for i in range(4):
            at = slice(i * wide, (i + 1) * wide)
            left = jnp.concatenate([lhs[k, :, at], lhs_in[:, at]], axis=0)
            both = jnp.concatenate([dlow[...], dlow_in[...]], axis=0)
            out = nn(left.T, both)
            for j in range(wide // DEEP):
                ez[i * (wide // DEEP) + j] = out[j * DEEP : (j + 1) * DEEP].astype(BF)
            plan.now += 0.4
            yield plan.now
        end = Join(2, lambda: plan.spawn(plane_sum(), plan.now))
        block, slot = cut(ez, DEEP // 2), cut(ez_in, DEEP // 2)
        for w, way in enumerate((1, -1)):
            plan.spawn(
                scatter_chain(
                    links,
                    "z",
                    way,
                    NZ,
                    z,
                    block,
                    lambda step, p, w=w: slot(w, step - 1, p),
                    at_z,
                    end.done,
                ),
                plan.now,
            )
        yield when
        meet.wait_recv()
        bz_in[z] = dbias[...] + dbias_in[...]
        bias_z.start()

    def plane_sum():
        yield plan.now
        bias_z.wait_recv()
        last = NZ // 2 - 1
        total = ez[z].astype(F32) + ez_in[0, last].astype(F32) + ez_in[1, last].astype(F32)
        low = bz_in[0]
        for i in range(1, NZ):
            low = low + bz_in[i]
        for j in range(NX):
            ex[j, 0:DEEP] = total[:, j * LANES : (j + 1) * LANES]
            ex[j, DEEP : DEEP + 8] = low
        ex_in[x] = ex[x]
        sum_x.start()
        yield plan.now + PLANE
        sum_x.wait_recv()
        total = ex_in[0]
        for i in range(1, NX):
            total = total + ex_in[i]
        for i in range(NY):
            ey[i, 0:8] = total[8 * i : 8 * i + 8]
            ey[i, 8:16] = total[DEEP : DEEP + 8]
        ey_in[y] = ey[y]
        sum_y.start()
        yield plan.now + PLANE
        sum_y.wait_recv()
        total = ey_in[0]
        for i in range(1, NY):
            total = total + ey_in[i]
        total = total * factor
        ag[y] = total[0:8]
        all_y.start()
        for j in range(WIDTH // LANES):
            gb[:, j * LANES : (j + 1) * LANES] = total[8 + j : 9 + j]
        yield plan.now + PLANE
        all_y.wait_recv()
        low = jnp.concatenate([ag[i] for i in range(NY)], axis=0).astype(BF)
        grads[k, z, :, lanes_of(x)] = low
        all_x.start()
        yield plan.now + PLANE
        all_x.wait_recv()
        mates = []
        end = Join(2, lambda: plan.spawn(collect(mates), max(when for _, when in mates)))
        view = cut(grads, DEEP // 2)

        def pass_on(o, p):
            ref = view(k, o, p)
            mates.append(links.start(ref, ref, partner, "core"))

        for way in (1, -1):
            chain = gather_chain(
                links,
                "z",
                way,
                NZ,
                z,
                lambda o, p: view(k, o, p),
                at_z,
                end.done,
                pass_on,
            )
            plan.spawn(chain, plan.now)

    def collect(mates):
        yield plan.now
        for copy, _ in mates:
            copy.wait_recv()

    factor = 1.0 / math.sqrt(ROWS * NR * NC)
    bias_z = Direct(links, NZ, z, at_z, lambda o: bz_in.at[z], lambda i: bz_in.at[i])
    sum_x = Direct(links, NX, x, at_x, lambda o: ex.at[o], lambda i: ex_in.at[i])
    sum_y = Direct(links, NY, y, at_y, lambda o: ey.at[o], lambda i: ey_in.at[i])
    all_y = Direct(links, NY, y, at_y, lambda o: ag.at[y], lambda i: ag.at[i])

    def lanes_of(i):
        return pl.ds(pl.multiple_of(i * LANES, LANES), LANES)

    all_x = Direct(
        links,
        NX,
        x,
        at_x,
        lambda o: grads.at[k, z, :, lanes_of(x)],
        lambda i: grads.at[k, z, :, lanes_of(i)],
    )

    ready_a = [Join(2 * (NX + NY), lambda q=q: plan.spawn(forward(q), plan.now)) for q in fwd]
    ready_b = Join(len(FWD), lambda: plan.spawn(middle(), plan.now))
    for q in fwd:
        plan.spawn(gather(q), STAGGER * q)
    plan.later(0.4, take_tiles)
    for m in range(SLOTS):
        plan.later(0.3, functools.partial(turn, m))
    plan.later(1.5, degrees)
    plan.later(1.0, self_term)
    plan.spawn(invert(), 2.0)
    plan.run()
    assert links.used <= SEMS

    stores = [
        pltpu.make_async_copy(gft, gfeat_out, local.at[16]),
        pltpu.make_async_copy(grads, grads_out, local.at[17]),
        pltpu.make_async_copy(gb, gbias_out, local.at[18]),
    ]
    for copy in stores:
        copy.start()
    links.finish()
    hidden_store.wait()
    for copy in stores:
        copy.wait()


def write_out(hidden, gfeat, grads, gbias, hidden_out, gfeat_out, gneigh_out, gself_out, gbias_out, *scratch):
    *held, sems = scratch
    sources = [grads.at[0], grads.at[1], hidden, gfeat, gbias]
    targets = [gneigh_out, gself_out, hidden_out, gfeat_out, gbias_out]
    count = len(held)
    takes = [pltpu.make_async_copy(a, b, sems.at[i]) for i, (a, b) in enumerate(zip(sources, held))]
    gives = [pltpu.make_async_copy(a, b, sems.at[count + i]) for i, (a, b) in enumerate(zip(held, targets))]
    for copy in takes:
        copy.start()
    for take, give in zip(takes, gives):
        take.wait()
        give.start()
    for copy in gives:
        copy.wait()


def on_device(
    features, tile_vals, tile_rows, tile_cols, tile_count, window, w_neigh, w_self, layer_bias, cotangent
):
    rows, width = features.shape
    slots, edge = tile_vals.shape[1:3]
    ny = lax.axis_size("row") // NX
    nz = lax.axis_size("col") // 2
    nc = 2 * nz

    def vmem(*shape, dtype=BF):
        return pltpu.VMEM(shape, dtype)

    fwd, bwd = [w for w, _ in FWD], [w for w, _ in BWD]
    each = [
        (fwd, (ny, NX, ROWS)),
        (fwd, (2, nz, ROWS)),
        (fwd, (nz, ROWS)),
        (fwd, (nz, ROWS)),
        (fwd, (slots + 1, edge)),
        (bwd, (nz, 2, ROWS)),
        (bwd, (slots + 1, edge)),
        (bwd, (ny, NX, ROWS)),
        (bwd, (2, ny // 2, NX, TOP_BWD)),
        (bwd, (NX, TOP_BWD)),
        (bwd, (2, NX // 2, ny, ROWS - TOP_BWD)),
        (bwd, (ny, ROWS - TOP_BWD)),
    ]
    deep = width // nz
    scratch = [vmem(*shape, w) for widths, shape in each for w in widths]
    scratch += [vmem(slots + 1, edge, edge)] * 2
    scratch += [vmem(rows, width), vmem(rows, width), vmem(width, width), vmem(width, width)]
    scratch += [vmem(1, width, dtype=F32)]
    scratch += [vmem(nc, 8, ROWS, dtype=F32)] * 2
    scratch += [vmem(ROWS, LANES, dtype=F32)] * 2
    scratch += [vmem(rows, width, dtype=F32)] * 2
    scratch += [vmem(2, rows, width), vmem(rows, width)]
    scratch += [vmem(rows, width)] * 2
    scratch += [vmem(8, LANES, dtype=F32)] * 2
    scratch += [vmem(nz, deep, width), vmem(2, nz // 2, deep, width)]
    scratch += [vmem(nz, 8, LANES, dtype=F32)]
    scratch += [vmem(NX, deep + 8, LANES, dtype=F32)] * 2
    scratch += [vmem(ny, 16, LANES, dtype=F32)] * 2
    scratch += [vmem(ny, 8, LANES, dtype=F32)]
    scratch += [vmem(2, nz, deep, width)]
    scratch += [vmem(rows, width)] * 2 + [vmem(1, width, dtype=F32)]
    scratch += [pltpu.SMEM(a.shape, jnp.int32) for a in (tile_rows, tile_cols, tile_count, window)]
    scratch += [pltpu.SemaphoreType.DMA((SEMS,))] * 2 + [pltpu.SemaphoreType.DMA((20,))]
    anywhere = pl.BlockSpec(memory_space=pl.ANY)
    far = pl.BlockSpec(memory_space=pltpu.HBM)
    sizes = (ny, nz, slots, edge, width)
    matrix = jax.ShapeDtypeStruct((rows, width), BF)
    weight = jax.ShapeDtypeStruct((nz, deep, width), BF)
    vector = jax.ShapeDtypeStruct((1, width), F32)
    results = pl.pallas_call(
        functools.partial(layer, sizes),
        out_shape=(matrix, matrix, jax.ShapeDtypeStruct((2, nz, deep, width), BF), vector),
        in_specs=[far] * 10,
        out_specs=(anywhere,) * 4,
        scratch_shapes=scratch,
        compiler_params=pltpu.CompilerParams(
            collective_id=0, has_side_effects=True, vmem_limit_bytes=VMEM_LIMIT
        ),
    )(
        features,
        tile_vals,
        tile_rows,
        tile_cols,
        tile_count,
        window,
        w_neigh,
        w_self,
        layer_bias.reshape(1, width),
        cotangent,
    )
    hidden, gfeat, gneigh, gself, gbias = pl.pallas_call(
        write_out,
        out_shape=(matrix, matrix, weight, weight, vector),
        in_specs=[anywhere] * 4,
        out_specs=(far,) * 5,
        scratch_shapes=[
            vmem(nz, deep, width),
            vmem(nz, deep, width),
            vmem(rows, width),
            vmem(rows, width),
            vmem(1, width, dtype=F32),
            pltpu.SemaphoreType.DMA((10,)),
        ],
        compiler_params=pltpu.CompilerParams(vmem_limit_bytes=VMEM_LIMIT),
    )(*results)
    return hidden, gfeat, gneigh.reshape(width, width), gself.reshape(width, width), gbias.reshape(width)


def solution(mesh):
    in_specs = (
        P(("col", "row"), None),
        P("row", "col", None, None),
        P("row", "col"),
        P("row", "col"),
        P("row", "col"),
        P("row", None),
        P(),
        P(),
        P(),
        P(("col", "row"), None),
    )
    out_specs = (P(("col", "row"), None), P(("col", "row"), None), P(), P(), P())
    return jax.shard_map(
        on_device, mesh=mesh, in_specs=in_specs, out_specs=out_specs, check_vma=False
    )
```

```python
import functools
import heapq
import math

import jax
import jax.numpy as jnp
from jax import lax
from jax.experimental import pallas as pl
from jax.experimental.pallas import tpu as pltpu
from jax.sharding import PartitionSpec as P

MESH = pl.DeviceIdType.MESH
BF = jnp.bfloat16
F32 = jnp.float32

NX = 4
FWD = ((256, False), (256, False),)
BWD = ((256, False), (256, False),)
STAGGER = 0
TOP_FWD, TOP_BWD = 48, 64
ROWS = 128
HALF = ROWS // 2
LANES = 128
SEMS = 480
VMEM_LIMIT = 63 * 1024 * 1024
LINK_RATE, HOP = 80e3, 2.8
CORE_RATE, CORE_HOP = 350e3, 0.9
ISSUE = 0.07
PLANE = 4.5


def nn(a, b):
    return jnp.dot(a, b, preferred_element_type=F32)


def nt(a, b):
    return lax.dot_general(a, b, (((1,), (1,)), ((), ())), preferred_element_type=F32)


class Plan:
    def __init__(self):
        self.heap, self.count, self.now, self.idle = [], 0, 0.0, []

    def spawn(self, chain, when):
        heapq.heappush(self.heap, (when, self.count, chain))
        self.count += 1

    def later(self, cost, work):
        self.idle.append((cost, work))

    def flush(self):
        while self.idle:
            cost, work = self.idle.pop(0)
            work()
            self.now += cost

    def run(self):
        while self.heap or self.idle:
            if self.idle and (not self.heap or self.heap[0][0] > self.now + self.idle[0][0]):
                cost, work = self.idle.pop(0)
                work()
                self.now += cost
                continue
            when, _, chain = heapq.heappop(self.heap)
            self.now = max(self.now, when)
            try:
                self.spawn(chain, next(chain))
            except StopIteration:
                pass


class Join:
    def __init__(self, count, then):
        self.count, self.then = count, then

    def done(self):
        self.count -= 1
        if self.count == 0:
            self.then()


class Links:
    def __init__(self, plan, send, recv):
        self.plan, self.send, self.recv, self.used, self.sent = plan, send, recv, 0, []
        self.free = {}

    def start(self, src, dst, device, link, hops=1):
        at = self.used
        self.used += 1
        copy = pltpu.make_async_remote_copy(
            src_ref=src,
            dst_ref=dst,
            send_sem=self.send.at[at],
            recv_sem=self.recv.at[at],
            device_id=device,
            device_id_type=MESH,
        )
        copy.start()
        self.sent.append(copy)
        size = math.prod(src.shape) * src.dtype.itemsize
        rate, hop = (CORE_RATE, CORE_HOP) if link == "core" else (LINK_RATE / 2, HOP)
        self.plan.now += ISSUE
        ready = max(self.plan.now, self.free.get(link, 0.0)) + hops * size / rate
        self.free[link] = ready
        return copy, ready + hop + 0.3 * (hops - 1)

    def finish(self):
        for copy in self.sent:
            copy.wait_send()


class Direct:
    def __init__(self, links, size, me, device, src, dst):
        self.links, self.size, self.me = links, size, me
        self.device, self.src, self.dst = device, src, dst
        self.base = links.used
        links.used += size - 1
        links.sent.append(self)

    def copy(self, step):
        other = lax.rem(self.me + step, self.size)
        return pltpu.make_async_remote_copy(
            src_ref=self.src(other),
            dst_ref=self.dst(self.me),
            send_sem=self.links.send.at[self.base + step - 1],
            recv_sem=self.links.recv.at[self.base + step - 1],
            device_id=self.device(other),
            device_id_type=MESH,
        )

    def start(self):
        @pl.loop(1, self.size)
        def _(step):
            self.copy(step).start()

        self.links.plan.now += ISSUE * self.size

    def wait_recv(self):
        @pl.loop(1, self.size)
        def _(step):
            self.copy(step).wait_recv()

    def wait_send(self):
        @pl.loop(1, self.size)
        def _(step):
            self.copy(step).wait_send()


def gather_chain(links, axis, way, size, me, block, device, done, pass_on=None):
    steps, held = size // 2, None
    half = 0 if way > 0 else 1
    for step in range(1, steps + 2):
        owner = lax.rem(me - way * (step - 1) + size, size)
        if held is not None:
            yield held[1]
            held[0].wait_recv()
        if step <= steps:
            ref = block(owner, None if step < steps else half)
            held = links.start(ref, ref, device(lax.rem(me + way + size, size)), (axis, way))
        if pass_on is not None and (step > 1 or way > 0):
            pass_on(owner, None if step <= steps else half)
    done()


def scatter_chain(links, axis, way, size, me, block, slot, device, done):
    steps, held = size // 2, None
    half = 0 if way > 0 else 1
    for step in range(1, steps + 1):
        owner = lax.rem(me + way * (steps - step + 1) + size, size)
        part = half if step == 1 else None
        if held is not None:
            yield held[1]
            held[0].wait_recv()
            was = half if step == 2 else None
            add_into(block(owner, was), slot(step - 1, was))
            links.plan.now += 0.2
        held = links.start(
            block(owner, part), slot(step, part), device(lax.rem(me + way + size, size)), (axis, way)
        )
    yield held[1]
    held[0].wait_recv()
    done()


def add_into(to, frm):
    to[...] = to[...] + frm[...]


def layer(
    sizes,
    feat,
    tiles,
    rows_in,
    cols_in,
    count_in,
    window_in,
    w_neigh,
    w_self,
    bias_in,
    cot,
    hidden_out,
    gfeat_out,
    grads_out,
    gbias_out,
    *scratch,
):
    names = list(scratch)

    def take():
        return names.pop(0)

    NY, NZ, SLOTS, EDGE, WIDTH = sizes
    NC, NR = 2 * NZ, NX * NY
    XH = NX // 2
    DEEP = WIDTH // NZ
    fwd, bwd = range(len(FWD)), range(len(BWD))
    fwd_at = [sum(w for w, _ in FWD[:q]) for q in fwd]
    bwd_at = [sum(w for w, _ in BWD[:q]) for q in bwd]
    panel = [take() for _ in fwd]
    part = [take() for _ in fwd]
    pair = [take() for _ in fwd]
    zslot = [take() for _ in fwd]
    prod = [take() for _ in fwd]
    back = [take() for _ in bwd]
    back_prod = [take() for _ in bwd]
    colp = [take() for _ in bwd]
    ry0 = [take() for _ in bwd]
    rx0 = [take() for _ in bwd]
    rx1 = [take() for _ in bwd]
    ry1 = [take() for _ in bwd]
    tile = take()
    turned = take()
    featv, cotv, wnv, wsv = take(), take(), take(), take()
    bias = take()
    deg_own, deg_all = take(), take()
    own_in, inv = take(), take()
    pre = take()
    selfg = take()
    lhs, lhs_in = take(), take()
    dlow, dlow_in = take(), take()
    dbias, dbias_in = take(), take()
    ez, ez_in = take(), take()
    bz_in = take()
    ex, ex_in = take(), take()
    ey, ey_in = take(), take()
    ag = take()
    grads = take()
    hid, gft, gb = take(), take(), take()
    tile_rows, tile_cols, tile_count, window = take(), take(), take(), take()
    send, recv, local = take(), take(), take()
    assert not names

    r, c = lax.axis_index("row"), lax.axis_index("col")
    y, x = r // NX, lax.rem(r, NX)
    z, k = c // 2, lax.rem(c, 2)
    mate = 1 - k

    def at_x(i):
        return {"row": y * NX + i}

    def at_y(i):
        return {"row": i * NX + x}

    def at_z(i):
        return {"col": i * 2 + k}

    def at_c(i):
        return {"col": i}

    partner = {"col": z * 2 + mate}

    loads = []

    def load(src, dst):
        copy = pltpu.make_async_copy(src, dst, local.at[len(loads)])
        copy.start()
        loads.append(copy)
        return copy

    barrier = pltpu.get_barrier_semaphore()

    @pl.loop(1, NX)
    def _(i):
        pl.semaphore_signal(barrier, inc=1, device_id=at_x(lax.rem(x + i, NX)), device_id_type=MESH)

    @pl.loop(1, NY)
    def _(i):
        pl.semaphore_signal(barrier, inc=1, device_id=at_y(lax.rem(y + i, NY)), device_id_type=MESH)

    @pl.loop(1, NC)
    def _(i):
        pl.semaphore_signal(barrier, inc=1, device_id=at_c(lax.rem(c + i, NC)), device_id_type=MESH)

    own = []
    for q in fwd:
        own.append(load(feat.at[:, pl.ds(fwd_at[q], FWD[q][0])], panel[q].at[y, x]))
    scalars = [
        load(rows_in, tile_rows),
        load(cols_in, tile_cols),
        load(count_in, tile_count),
        load(window_in, window),
    ]
    tile_load = load(tiles.at[0], tile.at[pl.ds(0, SLOTS)])
    feat_load = load(feat, featv)
    ws_load = load(w_self, wsv)
    bias_load = load(bias_in, bias)
    wn_load = load(w_neigh, wnv)
    cot_load = load(cot, cotv)
    for copy in own + scalars:
        copy.wait()

    pl.semaphore_wait(barrier, NX + NY + NC - 3)

    plan = Plan()
    links = Links(plan, send, recv)
    lo, hi = window[0, 0], window[0, 1]
    count = tile_count[0, 0]
    slot_row = [tile_rows[0, m] for m in range(SLOTS)]
    slot_col = [tile_cols[0, m] for m in range(SLOTS)]

    def slot_of(ids, want):
        found = jnp.int32(SLOTS)
        for m in range(SLOTS):
            found = jnp.where((ids[m] == want) & (m < count), m, found)
        return found

    def cut(ref, half):
        def view(*at):
            *lead, p = at
            if p is None:
                return ref.at[tuple(lead)]
            return ref.at[(*lead, pl.ds(half * p, half))]

        return view

    def far(d, size):
        d = d if d <= size // 2 else d - size
        return d, 1 if d > 0 else -1

    def straight(axis, size, me, device, src, dst):
        copies = []
        for d in sorted(range(1, size), key=lambda d: -abs(far(d, size)[0])):
            other = lax.rem(me + d, size)
            steps, way = far(d, size)
            copies.append(links.start(src(other), dst(me), device(other), (axis, way), abs(steps)))
        return copies

    def lanes_half(ref, at, p, wide):
        if p is None:
            return ref.at[at]
        return ref.at[(*at, pl.ds(p * (wide // 2), wide // 2))]

    def gather0(q):
        rows, wide = pl.ds(0, TOP_FWD), FWD[q][0]

        def along_y(b):
            for way in (1, -1):
                chain = gather_chain(
                    links,
                    "y",
                    way,
                    NY,
                    y,
                    lambda o, p: lanes_half(panel[q], (o, b, rows), p, wide),
                    at_y,
                    ready_a[q].done,
                )
                plan.spawn(chain, plan.now)

        halves = []

        def arrived(b, p):
            if p is not None:
                halves.append(b)
                if len(halves) < 2:
                    return
            along_y(b)

        for way in (1, -1):
            chain = gather_chain(
                links,
                "x",
                way,
                NX,
                x,
                lambda o, p: lanes_half(panel[q], (y, o, rows), p, wide),
                at_x,
                lambda: None,
                arrived,
            )
            plan.spawn(chain, plan.now)

    def gather1(q):
        rows, wide = pl.ds(TOP_FWD, ROWS - TOP_FWD), FWD[q][0]
        halves = []

        def along_x(b):
            for way in (1, -1):
                chain = gather_chain(
                    links,
                    "x",
                    way,
                    NX,
                    x,
                    lambda o, p: lanes_half(panel[q], (b, o, rows), p, wide),
                    at_x,
                    ready_a[q].done,
                )
                plan.spawn(chain, plan.now)

        def arrived(b, p):
            if p is not None:
                halves.append(b)
                if len(halves) < 2:
                    return
            along_x(b)

        for way in (1, -1):
            chain = gather_chain(
                links,
                "y",
                way,
                NY,
                y,
                lambda o, p: lanes_half(panel[q], (o, x, rows), p, wide),
                at_y,
                lambda: None,
                arrived,
            )
            plan.spawn(chain, plan.now)

    def gather(q):
        yield STAGGER * q
        gather0(q)
        gather1(q)

    def take_tiles():
        tile_load.wait()
        tile[SLOTS] = jnp.zeros((EDGE, EDGE), BF)
        turned[SLOTS] = jnp.zeros((EDGE, EDGE), BF)
        for q in fwd:
            prod[q][SLOTS] = jnp.zeros((EDGE, FWD[q][0]), BF)
        for q in bwd:
            back_prod[q][SLOTS] = jnp.zeros((EDGE, BWD[q][0]), BF)

    def turn(m):
        turned[m] = tile[m].T

    def degrees():
        lane = lax.broadcasted_iota(jnp.int32, (8, EDGE), 1)

        @pl.loop(0, NZ)
        def _(t):
            total = nn(jnp.ones((8, EDGE), BF), turned[slot_of(slot_row, t)])
            at = lane + t * EDGE
            total = jnp.where((at >= lo) & (at < hi), total, 0.0)
            deg_own[2 * t] = total[:, :ROWS]
            deg_own[2 * t + 1] = total[:, ROWS:]

        deg_all[c] = deg_own[c]
        degree.start()

    def self_term():
        feat_load.wait()
        ws_load.wait()
        bias_load.wait()
        pre[...] = nn(featv[...], wsv[...]) + bias[...]
        lhs[1] = featv[...]
        at = lax.broadcasted_iota(jnp.int32, (ROWS, LANES), 0) + c * ROWS
        own_in[...] = jnp.where((at >= lo) & (at < hi), 1.0, 0.0)

    def invert():
        yield 6.0
        plan.flush()
        yield 18.0
        degree.wait_recv()
        total = deg_all[0]
        for i in range(1, NC):
            total = total + deg_all[i]
        inverse = 1.0 / (1.0 + total)
        inv[...] = jnp.tile(inverse, (ROWS // 8, 1)).T
        wn_load.wait()
        cot_load.wait()
        plan.now += 0.5

    degree = Direct(links, NC, c, at_c, lambda o: deg_own.at[o], lambda i: deg_all.at[i])

    def forward(q):
        wide, direct = FWD[q]
        yield plan.now
        plan.flush()

        @pl.loop(0, SLOTS)
        def _(m):
            j = tile_cols[0, m]
            yy, xx = j // XH, lax.rem(j, XH) * 2
            prod[q][m] = nn(tile[m], panel[q][yy, pl.ds(xx, 2)].reshape(EDGE, wide)).astype(BF)

        end = Join(2, ready_b.done)
        swaps = {}
        order = [NZ // 2]
        for d in range(NZ // 2 - 1, 0, -1):
            order += [d, -d]
        order.append(0)
        for d in order:
            t = lax.rem(z + d + NZ, NZ)
            out = prod[q][slot_of(slot_row, t)]
            at = lax.broadcasted_iota(jnp.int32, (EDGE, wide), 0) + t * EDGE
            out = jnp.where((at >= lo) & (at < hi), out, jnp.zeros_like(out))
            part[q][0, t] = out[:ROWS]
            part[q][1, t] = out[ROWS:]
            swaps[d] = links.start(part[q].at[mate, t], pair[q].at[t], partner, "core")
            plan.now += 0.1

        def meet(d):
            copy, when = swaps.pop(d)
            yield when
            copy.wait_recv()
            t = lax.rem(z + d + NZ, NZ)
            pair[q][t] = pair[q][t] + part[q][k, t]

        def chain(way):
            steps, held = NZ // 2, None
            half = 0 if way > 0 else 1
            slot, block = cut(zslot[q], HALF), cut(pair[q], HALF)
            for step in range(1, steps + 1):
                d = way * (steps - step + 1)
                owner = lax.rem(z + d + NZ, NZ)
                if d in swaps:
                    yield from meet(d)
                now = half if step == 1 else None
                if held is not None:
                    yield held[1]
                    held[0].wait_recv()
                    was = half if step == 2 else None
                    add_into(block(owner, was), slot(half * steps + step - 2, was))
                    plan.now += 0.2
                held = links.start(
                    block(owner, now),
                    slot(half * steps + step - 1, now),
                    at_z(lax.rem(z + way + NZ, NZ)),
                    ("z", way),
                )
            yield held[1]
            held[0].wait_recv()
            if 0 in swaps:
                yield from meet(0)
            end.done()

        def direct_chain():
            copies = []
            for d in order:
                yield from meet(d)
                if d != 0:
                    way = 1 if d > 0 else -1
                    t = lax.rem(z + d + NZ, NZ)
                    copies.append(links.start(pair[q].at[t], zslot[q].at[z], at_z(t), ("z", way), abs(d)))
            yield max(when for _, when in copies)
            for copy, _ in copies:
                copy.wait_recv()
            ready_b.done()

        def ring():
            yield from meet(NZ // 2)
            for way in (1, -1):
                plan.spawn(chain(way), plan.now)

        if direct:
            plan.spawn(direct_chain(), plan.now)
        else:
            plan.spawn(ring(), plan.now)

    def middle():
        yield plan.now
        half = NZ // 2
        for q in fwd:
            wide, direct = FWD[q]
            total = pair[q][z].astype(F32)
            if direct:
                for d in range(1, NZ):
                    total = total + zslot[q][lax.rem(z + d, NZ)].astype(F32)
            else:
                total = total + zslot[q][half - 1].astype(F32) + zslot[q][2 * half - 1].astype(F32)
            low = (total * jnp.tile(inv[...], (1, wide // LANES))).astype(BF)
            cols = slice(fwd_at[q], fwd_at[q] + wide)
            lhs[0, :, cols] = low
            pre[...] += nn(low, wnv[cols, :])
        swaps = [links.start(lhs.at[mate], lhs_in, partner, "core")]
        value = pre[...]
        s = jax.nn.sigmoid(value)
        dpre = cotv[...].astype(F32) * (s * (1.0 + value * (1.0 - s)))
        low = dpre.astype(BF)
        dlow[...] = low
        swaps.append(links.start(dlow, dlow_in, partner, "core"))
        scale = inv[...] * own_in[...]
        plan.now += 1.5
        for q in bwd:
            wide = BWD[q][0]
            out = nt(low, wnv[bwd_at[q] : bwd_at[q] + wide, :]) * jnp.tile(scale, (1, wide // LANES))
            back[q][z, k] = out.astype(BF)
            plan.now += 0.4
            spread(q)
        total = jnp.sum(dpre, axis=0, keepdims=True)
        lanes = [total[:, i * LANES : (i + 1) * LANES] for i in range(WIDTH // LANES)]
        dbias[...] = jnp.concatenate(lanes + [jnp.zeros((8 - len(lanes), LANES), F32)], axis=0)
        hid[...] = (value * s).astype(BF)
        hidden_store.start()
        plan.now += 0.4
        plan.spawn(gradients(swaps), plan.now)

        def self_back():
            selfg[...] = nt(dlow[...], wsv[...])

        plan.later(0.7, self_back)

    hidden_store = pltpu.make_async_copy(hid, hidden_out, local.at[15])

    def spread(q):
        mates = []
        view = cut(back[q], HALF)

        def pass_on(o, p):
            ref = view(o, k, p)
            mates.append(links.start(ref, ref, partner, "core"))

        def then():
            plan.spawn(backward(q, mates), max(when for _, when in mates))

        def direct_chain():
            mine = back[q].at[z, k]
            pass_on(z, None)
            copies = []
            for d in sorted(range(1, NZ), key=lambda d: -abs(far(d, NZ)[0])):
                other = lax.rem(z + d, NZ)
                steps, way = far(d, NZ)
                copies.append((d, *links.start(mine, mine, at_z(other), ("z", way), abs(steps))))
            for d, copy, when in sorted(copies, key=lambda item: item[2]):
                yield when
                copy.wait_recv()
                pass_on(lax.rem(z - d + NZ, NZ), None)
            then()

        if BWD[q][1]:
            plan.spawn(direct_chain(), plan.now)
            return
        end = Join(2, then)
        for way in (1, -1):
            chain = gather_chain(
                links, "z", way, NZ, z, lambda o, p: view(o, k, p), at_z, end.done, pass_on
            )
            plan.spawn(chain, plan.now)

    def backward(q, mates):
        yield plan.now
        plan.flush()
        for copy, _ in mates:
            copy.wait_recv()
        wide = BWD[q][0]

        @pl.loop(0, SLOTS)
        def _(m):
            t = tile_rows[0, m]
            back_prod[q][m] = nn(turned[m], back[q][t].reshape(EDGE, wide)).astype(BF)

        @pl.loop(0, NY * XH)
        def _(j):
            out = back_prod[q][slot_of(slot_col, j)]
            yy, xx = j // XH, lax.rem(j, XH) * 2
            for i in range(2):
                colp[q][yy, xx + i] = out[i * ROWS : (i + 1) * ROWS]

        plan.now += 2.0
        scatter0(q)
        scatter1(q)

    top, low_rows = pl.ds(0, HALF), HALF // 2

    def scatter0(q):
        last_y = NY // 2 - 1

        def tail():
            copies = straight("x", NX, x, at_x, lambda o: colp[q].at[y, o, top], lambda i: rx0[q].at[i])
            yield max(when for _, when in copies)
            for copy, _ in copies:
                copy.wait_recv()
            write(q, 0, [rx0[q][lax.rem(x + d, NX)] for d in range(1, NX)])

        def then():
            for w in range(2):
                add_into(colp[q].at[y, :, top], ry0[q].at[w, last_y])
            plan.spawn(tail(), plan.now)

        def block(o, p):
            if p is None:
                return colp[q].at[o, :, top]
            return colp[q].at[o, pl.ds(XH * p, XH), top]

        mid = Join(2, then)
        slot = cut(ry0[q], XH)
        for w, way in enumerate((1, -1)):
            chain = scatter_chain(
                links, "y", way, NY, y, block, lambda step, p, w=w: slot(w, step - 1, p), at_y, mid.done
            )
            plan.spawn(chain, plan.now)

    def scatter1(q):
        last_y, last_x = NY // 2 - 1, NX // 2 - 1
        deep = NY // 2
        bottom = pl.ds(HALF, HALF)

        def finish():
            write(q, 1, [ry1[q][last_y], ry1[q][NY - 1]])

        def inner(o, p):
            if p is None:
                return colp[q].at[o, x, bottom]
            return colp[q].at[o, x, pl.ds(HALF + low_rows * p, low_rows)]

        def then():
            for w in range(2):
                add_into(colp[q].at[:, x, bottom], rx1[q].at[w, last_x])
            end = Join(2, finish)
            slot = cut(ry1[q], low_rows)
            for w, way in enumerate((1, -1)):
                chain = scatter_chain(
                    links,
                    "y",
                    way,
                    NY,
                    y,
                    inner,
                    lambda step, p, w=w: slot(w * (NY // 2) + step - 1, p),
                    at_y,
                    end.done,
                )
                plan.spawn(chain, plan.now)

        def block(o, p):
            if p is None:
                return colp[q].at[:, o, bottom]
            return colp[q].at[pl.ds(deep * p, deep), o, bottom]

        mid = Join(2, then)
        slot = cut(rx1[q], deep)
        for w, way in enumerate((1, -1)):
            chain = scatter_chain(
                links, "x", way, NX, x, block, lambda step, p, w=w: slot(w, step - 1, p), at_x, mid.done
            )
            plan.spawn(chain, plan.now)

    def write(q, h, terms):
        rows = slice(TOP_BWD, ROWS) if h else slice(0, TOP_BWD)
        cols = slice(bwd_at[q], bwd_at[q] + BWD[q][0])
        total = colp[q][y, x, rows].astype(F32)
        for term in terms:
            total = total + term.astype(F32)
        gft[rows, cols] = (total + selfg[rows, cols]).astype(BF)

    def gradients(swaps):
        meet, when = links.start(dbias, dbias_in, partner, "core")
        yield swaps[-1][1]
        for copy, _ in swaps:
            copy.wait_recv()
        wide = WIDTH // 4
        for i in range(4):
            at = slice(i * wide, (i + 1) * wide)
            left = jnp.concatenate([lhs[k, :, at], lhs_in[:, at]], axis=0)
            both = jnp.concatenate([dlow[...], dlow_in[...]], axis=0)
            out = nn(left.T, both)
            for j in range(wide // DEEP):
                ez[i * (wide // DEEP) + j] = out[j * DEEP : (j + 1) * DEEP].astype(BF)
            plan.now += 0.4
            yield plan.now
        end = Join(2, lambda: plan.spawn(plane_sum(), plan.now))
        block, slot = cut(ez, DEEP // 2), cut(ez_in, DEEP // 2)
        for w, way in enumerate((1, -1)):
            plan.spawn(
                scatter_chain(
                    links,
                    "z",
                    way,
                    NZ,
                    z,
                    block,
                    lambda step, p, w=w: slot(w, step - 1, p),
                    at_z,
                    end.done,
                ),
                plan.now,
            )
        yield when
        meet.wait_recv()
        bz_in[z] = dbias[...] + dbias_in[...]
        bias_z.start()

    def plane_sum():
        yield plan.now
        bias_z.wait_recv()
        last = NZ // 2 - 1
        total = ez[z].astype(F32) + ez_in[0, last].astype(F32) + ez_in[1, last].astype(F32)
        low = bz_in[0]
        for i in range(1, NZ):
            low = low + bz_in[i]
        for j in range(NX):
            ex[j, 0:DEEP] = total[:, j * LANES : (j + 1) * LANES]
            ex[j, DEEP : DEEP + 8] = low
        ex_in[x] = ex[x]
        sum_x.start()
        yield plan.now + PLANE
        sum_x.wait_recv()
        total = ex_in[0]
        for i in range(1, NX):
            total = total + ex_in[i]
        for i in range(NY):
            ey[i, 0:8] = total[8 * i : 8 * i + 8]
            ey[i, 8:16] = total[DEEP : DEEP + 8]
        ey_in[y] = ey[y]
        sum_y.start()
        yield plan.now + PLANE
        sum_y.wait_recv()
        total = ey_in[0]
        for i in range(1, NY):
            total = total + ey_in[i]
        total = total * factor
        ag[y] = total[0:8]
        all_y.start()
        for j in range(WIDTH // LANES):
            gb[:, j * LANES : (j + 1) * LANES] = total[8 + j : 9 + j]
        yield plan.now + PLANE
        all_y.wait_recv()
        low = jnp.concatenate([ag[i] for i in range(NY)], axis=0).astype(BF)
        grads[k, z, :, lanes_of(x)] = low
        all_x.start()
        yield plan.now + PLANE
        all_x.wait_recv()
        mates = []
        end = Join(2, lambda: plan.spawn(collect(mates), max(when for _, when in mates)))
        view = cut(grads, DEEP // 2)

        def pass_on(o, p):
            ref = view(k, o, p)
            mates.append(links.start(ref, ref, partner, "core"))

        for way in (1, -1):
            chain = gather_chain(
                links,
                "z",
                way,
                NZ,
                z,
                lambda o, p: view(k, o, p),
                at_z,
                end.done,
                pass_on,
            )
            plan.spawn(chain, plan.now)

    def collect(mates):
        yield plan.now
        for copy, _ in mates:
            copy.wait_recv()

    factor = 1.0 / math.sqrt(ROWS * NR * NC)
    bias_z = Direct(links, NZ, z, at_z, lambda o: bz_in.at[z], lambda i: bz_in.at[i])
    sum_x = Direct(links, NX, x, at_x, lambda o: ex.at[o], lambda i: ex_in.at[i])
    sum_y = Direct(links, NY, y, at_y, lambda o: ey.at[o], lambda i: ey_in.at[i])
    all_y = Direct(links, NY, y, at_y, lambda o: ag.at[y], lambda i: ag.at[i])

    def lanes_of(i):
        return pl.ds(pl.multiple_of(i * LANES, LANES), LANES)

    all_x = Direct(
        links,
        NX,
        x,
        at_x,
        lambda o: grads.at[k, z, :, lanes_of(x)],
        lambda i: grads.at[k, z, :, lanes_of(i)],
    )

    ready_a = [Join(2 * (NX + NY), lambda q=q: plan.spawn(forward(q), plan.now)) for q in fwd]
    ready_b = Join(len(FWD), lambda: plan.spawn(middle(), plan.now))
    for q in fwd:
        plan.spawn(gather(q), STAGGER * q)
    plan.later(0.4, take_tiles)
    for m in range(SLOTS):
        plan.later(0.3, functools.partial(turn, m))
    plan.later(1.5, degrees)
    plan.later(1.0, self_term)
    plan.spawn(invert(), 2.0)
    plan.run()
    assert links.used <= SEMS

    stores = [
        pltpu.make_async_copy(gft, gfeat_out, local.at[16]),
        pltpu.make_async_copy(grads, grads_out, local.at[17]),
        pltpu.make_async_copy(gb, gbias_out, local.at[18]),
    ]
    for copy in stores:
        copy.start()
    links.finish()
    hidden_store.wait()
    for copy in stores:
        copy.wait()


def write_out(hidden, gfeat, grads, gbias, hidden_out, gfeat_out, gneigh_out, gself_out, gbias_out, *scratch):
    *held, sems = scratch
    sources = [grads.at[0], grads.at[1], hidden, gfeat, gbias]
    targets = [gneigh_out, gself_out, hidden_out, gfeat_out, gbias_out]
    count = len(held)
    takes = [pltpu.make_async_copy(a, b, sems.at[i]) for i, (a, b) in enumerate(zip(sources, held))]
    gives = [pltpu.make_async_copy(a, b, sems.at[count + i]) for i, (a, b) in enumerate(zip(held, targets))]
    for copy in takes:
        copy.start()
    for take, give in zip(takes, gives):
        take.wait()
        give.start()
    for copy in gives:
        copy.wait()


def on_device(
    features, tile_vals, tile_rows, tile_cols, tile_count, window, w_neigh, w_self, layer_bias, cotangent
):
    rows, width = features.shape
    slots, edge = tile_vals.shape[1:3]
    ny = lax.axis_size("row") // NX
    nz = lax.axis_size("col") // 2
    nc = 2 * nz

    def vmem(*shape, dtype=BF):
        return pltpu.VMEM(shape, dtype)

    fwd, bwd = [w for w, _ in FWD], [w for w, _ in BWD]
    each = [
        (fwd, (ny, NX, ROWS)),
        (fwd, (2, nz, ROWS)),
        (fwd, (nz, ROWS)),
        (fwd, (nz, ROWS)),
        (fwd, (slots + 1, edge)),
        (bwd, (nz, 2, ROWS)),
        (bwd, (slots + 1, edge)),
        (bwd, (ny, NX, ROWS)),
        (bwd, (2, ny // 2, NX, TOP_BWD)),
        (bwd, (NX, TOP_BWD)),
        (bwd, (2, NX // 2, ny, ROWS - TOP_BWD)),
        (bwd, (ny, ROWS - TOP_BWD)),
    ]
    deep = width // nz
    scratch = [vmem(*shape, w) for widths, shape in each for w in widths]
    scratch += [vmem(slots + 1, edge, edge)] * 2
    scratch += [vmem(rows, width), vmem(rows, width), vmem(width, width), vmem(width, width)]
    scratch += [vmem(1, width, dtype=F32)]
    scratch += [vmem(nc, 8, ROWS, dtype=F32)] * 2
    scratch += [vmem(ROWS, LANES, dtype=F32)] * 2
    scratch += [vmem(rows, width, dtype=F32)] * 2
    scratch += [vmem(2, rows, width), vmem(rows, width)]
    scratch += [vmem(rows, width)] * 2
    scratch += [vmem(8, LANES, dtype=F32)] * 2
    scratch += [vmem(nz, deep, width), vmem(2, nz // 2, deep, width)]
    scratch += [vmem(nz, 8, LANES, dtype=F32)]
    scratch += [vmem(NX, deep + 8, LANES, dtype=F32)] * 2
    scratch += [vmem(ny, 16, LANES, dtype=F32)] * 2
    scratch += [vmem(ny, 8, LANES, dtype=F32)]
    scratch += [vmem(2, nz, deep, width)]
    scratch += [vmem(rows, width)] * 2 + [vmem(1, width, dtype=F32)]
    scratch += [pltpu.SMEM(a.shape, jnp.int32) for a in (tile_rows, tile_cols, tile_count, window)]
    scratch += [pltpu.SemaphoreType.DMA((SEMS,))] * 2 + [pltpu.SemaphoreType.DMA((20,))]
    anywhere = pl.BlockSpec(memory_space=pl.ANY)
    far = pl.BlockSpec(memory_space=pltpu.HBM)
    sizes = (ny, nz, slots, edge, width)
    matrix = jax.ShapeDtypeStruct((rows, width), BF)
    weight = jax.ShapeDtypeStruct((nz, deep, width), BF)
    vector = jax.ShapeDtypeStruct((1, width), F32)
    results = pl.pallas_call(
        functools.partial(layer, sizes),
        out_shape=(matrix, matrix, jax.ShapeDtypeStruct((2, nz, deep, width), BF), vector),
        in_specs=[far] * 10,
        out_specs=(anywhere,) * 4,
        scratch_shapes=scratch,
        compiler_params=pltpu.CompilerParams(
            collective_id=0, has_side_effects=True, vmem_limit_bytes=VMEM_LIMIT
        ),
    )(
        features,
        tile_vals,
        tile_rows,
        tile_cols,
        tile_count,
        window,
        w_neigh,
        w_self,
        layer_bias.reshape(1, width),
        cotangent,
    )
    hidden, gfeat, gneigh, gself, gbias = pl.pallas_call(
        write_out,
        out_shape=(matrix, matrix, weight, weight, vector),
        in_specs=[anywhere] * 4,
        out_specs=(far,) * 5,
        scratch_shapes=[
            vmem(nz, deep, width),
            vmem(nz, deep, width),
            vmem(rows, width),
            vmem(rows, width),
            vmem(1, width, dtype=F32),
            pltpu.SemaphoreType.DMA((10,)),
        ],
        compiler_params=pltpu.CompilerParams(vmem_limit_bytes=VMEM_LIMIT),
    )(*results)
    return hidden, gfeat, gneigh.reshape(width, width), gself.reshape(width, width), gbias.reshape(width)


def solution(mesh):
    in_specs = (
        P(("col", "row"), None),
        P("row", "col", None, None),
        P("row", "col"),
        P("row", "col"),
        P("row", "col"),
        P("row", None),
        P(),
        P(),
        P(),
        P(("col", "row"), None),
    )
    out_specs = (P(("col", "row"), None), P(("col", "row"), None), P(), P(), P())
    return jax.shard_map(
        on_device, mesh=mesh, in_specs=in_specs, out_specs=out_specs, check_vma=False
    )
```

```python
import functools
import heapq
import math

import jax
import jax.numpy as jnp
from jax import lax
from jax.experimental import pallas as pl
from jax.experimental.pallas import tpu as pltpu
from jax.sharding import PartitionSpec as P

MESH = pl.DeviceIdType.MESH
BF = jnp.bfloat16
F32 = jnp.float32

NX = 4
FWD = ((256, False), (256, False),)
BWD = ((256, False), (256, False),)
STAGGER = 0
TOP_FWD, TOP_BWD = 48, 64
ROWS = 128
HALF = ROWS // 2
LANES = 128
SEMS = 480
VMEM_LIMIT = 63 * 1024 * 1024
LINK_RATE, HOP = 80e3, 3.0
CORE_RATE, CORE_HOP = 350e3, 0.9
ISSUE = 0.07
PLANE = 5.0


def nn(a, b):
    return jnp.dot(a, b, preferred_element_type=F32)


def nt(a, b):
    return lax.dot_general(a, b, (((1,), (1,)), ((), ())), preferred_element_type=F32)


class Plan:
    def __init__(self):
        self.heap, self.count, self.now, self.idle = [], 0, 0.0, []

    def spawn(self, chain, when):
        heapq.heappush(self.heap, (when, self.count, chain))
        self.count += 1

    def later(self, cost, work):
        self.idle.append((cost, work))

    def flush(self):
        while self.idle:
            cost, work = self.idle.pop(0)
            work()
            self.now += cost

    def run(self):
        while self.heap or self.idle:
            if self.idle and (not self.heap or self.heap[0][0] > self.now + self.idle[0][0]):
                cost, work = self.idle.pop(0)
                work()
                self.now += cost
                continue
            when, _, chain = heapq.heappop(self.heap)
            self.now = max(self.now, when)
            try:
                self.spawn(chain, next(chain))
            except StopIteration:
                pass


class Join:
    def __init__(self, count, then):
        self.count, self.then = count, then

    def done(self):
        self.count -= 1
        if self.count == 0:
            self.then()


class Links:
    def __init__(self, plan, send, recv):
        self.plan, self.send, self.recv, self.used, self.sent = plan, send, recv, 0, []
        self.free = {}

    def start(self, src, dst, device, link, hops=1):
        at = self.used
        self.used += 1
        copy = pltpu.make_async_remote_copy(
            src_ref=src,
            dst_ref=dst,
            send_sem=self.send.at[at],
            recv_sem=self.recv.at[at],
            device_id=device,
            device_id_type=MESH,
        )
        copy.start()
        self.sent.append(copy)
        size = math.prod(src.shape) * src.dtype.itemsize
        rate, hop = (CORE_RATE, CORE_HOP) if link == "core" else (LINK_RATE / 2, HOP)
        self.plan.now += ISSUE
        ready = max(self.plan.now, self.free.get(link, 0.0)) + hops * size / rate
        self.free[link] = ready
        return copy, ready + hop + 0.3 * (hops - 1)

    def finish(self):
        for copy in self.sent:
            copy.wait_send()


class Direct:
    def __init__(self, links, size, me, device, src, dst):
        self.links, self.size, self.me = links, size, me
        self.device, self.src, self.dst = device, src, dst
        self.base = links.used
        links.used += size - 1
        links.sent.append(self)

    def copy(self, step):
        other = lax.rem(self.me + step, self.size)
        return pltpu.make_async_remote_copy(
            src_ref=self.src(other),
            dst_ref=self.dst(self.me),
            send_sem=self.links.send.at[self.base + step - 1],
            recv_sem=self.links.recv.at[self.base + step - 1],
            device_id=self.device(other),
            device_id_type=MESH,
        )

    def start(self):
        @pl.loop(1, self.size)
        def _(step):
            self.copy(step).start()

        self.links.plan.now += ISSUE * self.size

    def wait_recv(self):
        @pl.loop(1, self.size)
        def _(step):
            self.copy(step).wait_recv()

    def wait_send(self):
        @pl.loop(1, self.size)
        def _(step):
            self.copy(step).wait_send()


def gather_chain(links, axis, way, size, me, block, device, done, pass_on=None):
    steps, held = size // 2, None
    half = 0 if way > 0 else 1
    for step in range(1, steps + 2):
        owner = lax.rem(me - way * (step - 1) + size, size)
        if held is not None:
            yield held[1]
            held[0].wait_recv()
        if step <= steps:
            ref = block(owner, None if step < steps else half)
            held = links.start(ref, ref, device(lax.rem(me + way + size, size)), (axis, way))
        if pass_on is not None and (step > 1 or way > 0):
            pass_on(owner, None if step <= steps else half)
    done()


def scatter_chain(links, axis, way, size, me, block, slot, device, done):
    steps, held = size // 2, None
    half = 0 if way > 0 else 1
    for step in range(1, steps + 1):
        owner = lax.rem(me + way * (steps - step + 1) + size, size)
        part = half if step == 1 else None
        if held is not None:
            yield held[1]
            held[0].wait_recv()
            was = half if step == 2 else None
            add_into(block(owner, was), slot(step - 1, was))
            links.plan.now += 0.2
        held = links.start(
            block(owner, part), slot(step, part), device(lax.rem(me + way + size, size)), (axis, way)
        )
    yield held[1]
    held[0].wait_recv()
    done()


def add_into(to, frm):
    to[...] = to[...] + frm[...]


def layer(
    sizes,
    feat,
    tiles,
    rows_in,
    cols_in,
    count_in,
    window_in,
    w_neigh,
    w_self,
    bias_in,
    cot,
    hidden_out,
    gfeat_out,
    grads_out,
    gbias_out,
    *scratch,
):
    names = list(scratch)

    def take():
        return names.pop(0)

    NY, NZ, SLOTS, EDGE, WIDTH = sizes
    NC, NR = 2 * NZ, NX * NY
    XH = NX // 2
    DEEP = WIDTH // NZ
    fwd, bwd = range(len(FWD)), range(len(BWD))
    fwd_at = [sum(w for w, _ in FWD[:q]) for q in fwd]
    bwd_at = [sum(w for w, _ in BWD[:q]) for q in bwd]
    panel = [take() for _ in fwd]
    part = [take() for _ in fwd]
    pair = [take() for _ in fwd]
    zslot = [take() for _ in fwd]
    prod = [take() for _ in fwd]
    back = [take() for _ in bwd]
    back_prod = [take() for _ in bwd]
    colp = [take() for _ in bwd]
    ry0 = [take() for _ in bwd]
    rx0 = [take() for _ in bwd]
    rx1 = [take() for _ in bwd]
    ry1 = [take() for _ in bwd]
    tile = take()
    turned = take()
    featv, cotv, wnv, wsv = take(), take(), take(), take()
    bias = take()
    deg_own, deg_all = take(), take()
    own_in, inv = take(), take()
    pre = take()
    selfg = take()
    lhs, lhs_in = take(), take()
    dlow, dlow_in = take(), take()
    dbias, dbias_in = take(), take()
    ez, ez_in = take(), take()
    bz_in = take()
    ex, ex_in = take(), take()
    ey, ey_in = take(), take()
    ag = take()
    grads = take()
    hid, gft, gb = take(), take(), take()
    tile_rows, tile_cols, tile_count, window = take(), take(), take(), take()
    send, recv, local = take(), take(), take()
    assert not names

    r, c = lax.axis_index("row"), lax.axis_index("col")
    y, x = r // NX, lax.rem(r, NX)
    z, k = c // 2, lax.rem(c, 2)
    mate = 1 - k

    def at_x(i):
        return {"row": y * NX + i}

    def at_y(i):
        return {"row": i * NX + x}

    def at_z(i):
        return {"col": i * 2 + k}

    def at_c(i):
        return {"col": i}

    partner = {"col": z * 2 + mate}

    loads = []

    def load(src, dst):
        copy = pltpu.make_async_copy(src, dst, local.at[len(loads)])
        copy.start()
        loads.append(copy)
        return copy

    barrier = pltpu.get_barrier_semaphore()

    @pl.loop(1, NX)
    def _(i):
        pl.semaphore_signal(barrier, inc=1, device_id=at_x(lax.rem(x + i, NX)), device_id_type=MESH)

    @pl.loop(1, NY)
    def _(i):
        pl.semaphore_signal(barrier, inc=1, device_id=at_y(lax.rem(y + i, NY)), device_id_type=MESH)

    @pl.loop(1, NC)
    def _(i):
        pl.semaphore_signal(barrier, inc=1, device_id=at_c(lax.rem(c + i, NC)), device_id_type=MESH)

    own = []
    for q in fwd:
        own.append(load(feat.at[:, pl.ds(fwd_at[q], FWD[q][0])], panel[q].at[y, x]))
    scalars = [
        load(rows_in, tile_rows),
        load(cols_in, tile_cols),
        load(count_in, tile_count),
        load(window_in, window),
    ]
    tile_load = load(tiles.at[0], tile.at[pl.ds(0, SLOTS)])
    feat_load = load(feat, featv)
    ws_load = load(w_self, wsv)
    bias_load = load(bias_in, bias)
    wn_load = load(w_neigh, wnv)
    cot_load = load(cot, cotv)
    for copy in own + scalars:
        copy.wait()

    pl.semaphore_wait(barrier, NX + NY + NC - 3)

    plan = Plan()
    links = Links(plan, send, recv)
    lo, hi = window[0, 0], window[0, 1]
    count = tile_count[0, 0]
    slot_row = [tile_rows[0, m] for m in range(SLOTS)]
    slot_col = [tile_cols[0, m] for m in range(SLOTS)]

    def slot_of(ids, want):
        found = jnp.int32(SLOTS)
        for m in range(SLOTS):
            found = jnp.where((ids[m] == want) & (m < count), m, found)
        return found

    def cut(ref, half):
        def view(*at):
            *lead, p = at
            if p is None:
                return ref.at[tuple(lead)]
            return ref.at[(*lead, pl.ds(half * p, half))]

        return view

    def far(d, size):
        d = d if d <= size // 2 else d - size
        return d, 1 if d > 0 else -1

    def straight(axis, size, me, device, src, dst):
        copies = []
        for d in sorted(range(1, size), key=lambda d: -abs(far(d, size)[0])):
            other = lax.rem(me + d, size)
            steps, way = far(d, size)
            copies.append(links.start(src(other), dst(me), device(other), (axis, way), abs(steps)))
        return copies

    def lanes_half(ref, at, p, wide):
        if p is None:
            return ref.at[at]
        return ref.at[(*at, pl.ds(p * (wide // 2), wide // 2))]

    def gather0(q):
        rows, wide = pl.ds(0, TOP_FWD), FWD[q][0]

        def along_y(b):
            for way in (1, -1):
                chain = gather_chain(
                    links,
                    "y",
                    way,
                    NY,
                    y,
                    lambda o, p: lanes_half(panel[q], (o, b, rows), p, wide),
                    at_y,
                    ready_a[q].done,
                )
                plan.spawn(chain, plan.now)

        halves = []

        def arrived(b, p):
            if p is not None:
                halves.append(b)
                if len(halves) < 2:
                    return
            along_y(b)

        for way in (1, -1):
            chain = gather_chain(
                links,
                "x",
                way,
                NX,
                x,
                lambda o, p: lanes_half(panel[q], (y, o, rows), p, wide),
                at_x,
                lambda: None,
                arrived,
            )
            plan.spawn(chain, plan.now)

    def gather1(q):
        rows, wide = pl.ds(TOP_FWD, ROWS - TOP_FWD), FWD[q][0]
        halves = []

        def along_x(b):
            for way in (1, -1):
                chain = gather_chain(
                    links,
                    "x",
                    way,
                    NX,
                    x,
                    lambda o, p: lanes_half(panel[q], (b, o, rows), p, wide),
                    at_x,
                    ready_a[q].done,
                )
                plan.spawn(chain, plan.now)

        def arrived(b, p):
            if p is not None:
                halves.append(b)
                if len(halves) < 2:
                    return
            along_x(b)

        for way in (1, -1):
            chain = gather_chain(
                links,
                "y",
                way,
                NY,
                y,
                lambda o, p: lanes_half(panel[q], (o, x, rows), p, wide),
                at_y,
                lambda: None,
                arrived,
            )
            plan.spawn(chain, plan.now)

    def gather(q):
        yield STAGGER * q
        gather0(q)
        gather1(q)

    def take_tiles():
        tile_load.wait()
        tile[SLOTS] = jnp.zeros((EDGE, EDGE), BF)
        turned[SLOTS] = jnp.zeros((EDGE, EDGE), BF)
        for q in fwd:
            prod[q][SLOTS] = jnp.zeros((EDGE, FWD[q][0]), BF)
        for q in bwd:
            back_prod[q][SLOTS] = jnp.zeros((EDGE, BWD[q][0]), BF)

    def turn(m):
        turned[m] = tile[m].T

    def degrees():
        lane = lax.broadcasted_iota(jnp.int32, (8, EDGE), 1)

        @pl.loop(0, NZ)
        def _(t):
            total = nn(jnp.ones((8, EDGE), BF), turned[slot_of(slot_row, t)])
            at = lane + t * EDGE
            total = jnp.where((at >= lo) & (at < hi), total, 0.0)
            deg_own[2 * t] = total[:, :ROWS]
            deg_own[2 * t + 1] = total[:, ROWS:]

        deg_all[c] = deg_own[c]
        degree.start()

    def self_term():
        feat_load.wait()
        ws_load.wait()
        bias_load.wait()
        pre[...] = nn(featv[...], wsv[...]) + bias[...]
        lhs[1] = featv[...]
        at = lax.broadcasted_iota(jnp.int32, (ROWS, LANES), 0) + c * ROWS
        own_in[...] = jnp.where((at >= lo) & (at < hi), 1.0, 0.0)

    def invert():
        yield 6.0
        plan.flush()
        yield 18.0
        degree.wait_recv()
        total = deg_all[0]
        for i in range(1, NC):
            total = total + deg_all[i]
        inverse = 1.0 / (1.0 + total)
        inv[...] = jnp.tile(inverse, (ROWS // 8, 1)).T
        wn_load.wait()
        cot_load.wait()
        plan.now += 0.5

    degree = Direct(links, NC, c, at_c, lambda o: deg_own.at[o], lambda i: deg_all.at[i])

    def forward(q):
        wide, direct = FWD[q]
        yield plan.now
        plan.flush()

        @pl.loop(0, SLOTS)
        def _(m):
            j = tile_cols[0, m]
            yy, xx = j // XH, lax.rem(j, XH) * 2
            prod[q][m] = nn(tile[m], panel[q][yy, pl.ds(xx, 2)].reshape(EDGE, wide)).astype(BF)

        end = Join(2, ready_b.done)
        swaps = {}
        order = [NZ // 2]
        for d in range(NZ // 2 - 1, 0, -1):
            order += [d, -d]
        order.append(0)
        for d in order:
            t = lax.rem(z + d + NZ, NZ)
            out = prod[q][slot_of(slot_row, t)]
            at = lax.broadcasted_iota(jnp.int32, (EDGE, wide), 0) + t * EDGE
            out = jnp.where((at >= lo) & (at < hi), out, jnp.zeros_like(out))
            part[q][0, t] = out[:ROWS]
            part[q][1, t] = out[ROWS:]
            swaps[d] = links.start(part[q].at[mate, t], pair[q].at[t], partner, "core")
            plan.now += 0.1

        def meet(d):
            copy, when = swaps.pop(d)
            yield when
            copy.wait_recv()
            t = lax.rem(z + d + NZ, NZ)
            pair[q][t] = pair[q][t] + part[q][k, t]

        def chain(way):
            steps, held = NZ // 2, None
            half = 0 if way > 0 else 1
            slot, block = cut(zslot[q], HALF), cut(pair[q], HALF)
            for step in range(1, steps + 1):
                d = way * (steps - step + 1)
                owner = lax.rem(z + d + NZ, NZ)
                if d in swaps:
                    yield from meet(d)
                now = half if step == 1 else None
                if held is not None:
                    yield held[1]
                    held[0].wait_recv()
                    was = half if step == 2 else None
                    add_into(block(owner, was), slot(half * steps + step - 2, was))
                    plan.now += 0.2
                held = links.start(
                    block(owner, now),
                    slot(half * steps + step - 1, now),
                    at_z(lax.rem(z + way + NZ, NZ)),
                    ("z", way),
                )
            yield held[1]
            held[0].wait_recv()
            if 0 in swaps:
                yield from meet(0)
            end.done()

        def direct_chain():
            copies = []
            for d in order:
                yield from meet(d)
                if d != 0:
                    way = 1 if d > 0 else -1
                    t = lax.rem(z + d + NZ, NZ)
                    copies.append(links.start(pair[q].at[t], zslot[q].at[z], at_z(t), ("z", way), abs(d)))
            yield max(when for _, when in copies)
            for copy, _ in copies:
                copy.wait_recv()
            ready_b.done()

        def ring():
            yield from meet(NZ // 2)
            for way in (1, -1):
                plan.spawn(chain(way), plan.now)

        if direct:
            plan.spawn(direct_chain(), plan.now)
        else:
            plan.spawn(ring(), plan.now)

    def middle():
        yield plan.now
        half = NZ // 2
        for q in fwd:
            wide, direct = FWD[q]
            total = pair[q][z].astype(F32)
            if direct:
                for d in range(1, NZ):
                    total = total + zslot[q][lax.rem(z + d, NZ)].astype(F32)
            else:
                total = total + zslot[q][half - 1].astype(F32) + zslot[q][2 * half - 1].astype(F32)
            low = (total * jnp.tile(inv[...], (1, wide // LANES))).astype(BF)
            cols = slice(fwd_at[q], fwd_at[q] + wide)
            lhs[0, :, cols] = low
            pre[...] += nn(low, wnv[cols, :])
        swaps = [links.start(lhs.at[mate], lhs_in, partner, "core")]
        value = pre[...]
        s = jax.nn.sigmoid(value)
        dpre = cotv[...].astype(F32) * (s * (1.0 + value * (1.0 - s)))
        low = dpre.astype(BF)
        dlow[...] = low
        swaps.append(links.start(dlow, dlow_in, partner, "core"))
        scale = inv[...] * own_in[...]
        plan.now += 1.5
        for q in bwd:
            wide = BWD[q][0]
            out = nt(low, wnv[bwd_at[q] : bwd_at[q] + wide, :]) * jnp.tile(scale, (1, wide // LANES))
            back[q][z, k] = out.astype(BF)
            plan.now += 0.4
            spread(q)
        total = jnp.sum(dpre, axis=0, keepdims=True)
        lanes = [total[:, i * LANES : (i + 1) * LANES] for i in range(WIDTH // LANES)]
        dbias[...] = jnp.concatenate(lanes + [jnp.zeros((8 - len(lanes), LANES), F32)], axis=0)
        hid[...] = (value * s).astype(BF)
        hidden_store.start()
        plan.now += 0.4
        plan.spawn(gradients(swaps), plan.now)

        def self_back():
            selfg[...] = nt(dlow[...], wsv[...])

        plan.later(0.7, self_back)

    hidden_store = pltpu.make_async_copy(hid, hidden_out, local.at[15])

    def spread(q):
        mates = []
        view = cut(back[q], HALF)

        def pass_on(o, p):
            ref = view(o, k, p)
            mates.append(links.start(ref, ref, partner, "core"))

        def then():
            plan.spawn(backward(q, mates), max(when for _, when in mates))

        def direct_chain():
            mine = back[q].at[z, k]
            pass_on(z, None)
            copies = []
            for d in sorted(range(1, NZ), key=lambda d: -abs(far(d, NZ)[0])):
                other = lax.rem(z + d, NZ)
                steps, way = far(d, NZ)
                copies.append((d, *links.start(mine, mine, at_z(other), ("z", way), abs(steps))))
            for d, copy, when in sorted(copies, key=lambda item: item[2]):
                yield when
                copy.wait_recv()
                pass_on(lax.rem(z - d + NZ, NZ), None)
            then()

        if BWD[q][1]:
            plan.spawn(direct_chain(), plan.now)
            return
        end = Join(2, then)
        for way in (1, -1):
            chain = gather_chain(
                links, "z", way, NZ, z, lambda o, p: view(o, k, p), at_z, end.done, pass_on
            )
            plan.spawn(chain, plan.now)

    def backward(q, mates):
        yield plan.now
        plan.flush()
        for copy, _ in mates:
            copy.wait_recv()
        wide = BWD[q][0]

        @pl.loop(0, SLOTS)
        def _(m):
            t = tile_rows[0, m]
            back_prod[q][m] = nn(turned[m], back[q][t].reshape(EDGE, wide)).astype(BF)

        @pl.loop(0, NY * XH)
        def _(j):
            out = back_prod[q][slot_of(slot_col, j)]
            yy, xx = j // XH, lax.rem(j, XH) * 2
            for i in range(2):
                colp[q][yy, xx + i] = out[i * ROWS : (i + 1) * ROWS]

        plan.now += 2.0
        scatter0(q)
        scatter1(q)

    top, low_rows = pl.ds(0, HALF), HALF // 2

    def scatter0(q):
        last_y = NY // 2 - 1

        def tail():
            copies = straight("x", NX, x, at_x, lambda o: colp[q].at[y, o, top], lambda i: rx0[q].at[i])
            yield max(when for _, when in copies)
            for copy, _ in copies:
                copy.wait_recv()
            write(q, 0, [rx0[q][lax.rem(x + d, NX)] for d in range(1, NX)])

        def then():
            for w in range(2):
                add_into(colp[q].at[y, :, top], ry0[q].at[w, last_y])
            plan.spawn(tail(), plan.now)

        def block(o, p):
            if p is None:
                return colp[q].at[o, :, top]
            return colp[q].at[o, pl.ds(XH * p, XH), top]

        mid = Join(2, then)
        slot = cut(ry0[q], XH)
        for w, way in enumerate((1, -1)):
            chain = scatter_chain(
                links, "y", way, NY, y, block, lambda step, p, w=w: slot(w, step - 1, p), at_y, mid.done
            )
            plan.spawn(chain, plan.now)

    def scatter1(q):
        last_y, last_x = NY // 2 - 1, NX // 2 - 1
        deep = NY // 2
        bottom = pl.ds(HALF, HALF)

        def finish():
            write(q, 1, [ry1[q][last_y], ry1[q][NY - 1]])

        def inner(o, p):
            if p is None:
                return colp[q].at[o, x, bottom]
            return colp[q].at[o, x, pl.ds(HALF + low_rows * p, low_rows)]

        def then():
            for w in range(2):
                add_into(colp[q].at[:, x, bottom], rx1[q].at[w, last_x])
            end = Join(2, finish)
            slot = cut(ry1[q], low_rows)
            for w, way in enumerate((1, -1)):
                chain = scatter_chain(
                    links,
                    "y",
                    way,
                    NY,
                    y,
                    inner,
                    lambda step, p, w=w: slot(w * (NY // 2) + step - 1, p),
                    at_y,
                    end.done,
                )
                plan.spawn(chain, plan.now)

        def block(o, p):
            if p is None:
                return colp[q].at[:, o, bottom]
            return colp[q].at[pl.ds(deep * p, deep), o, bottom]

        mid = Join(2, then)
        slot = cut(rx1[q], deep)
        for w, way in enumerate((1, -1)):
            chain = scatter_chain(
                links, "x", way, NX, x, block, lambda step, p, w=w: slot(w, step - 1, p), at_x, mid.done
            )
            plan.spawn(chain, plan.now)

    def write(q, h, terms):
        rows = slice(TOP_BWD, ROWS) if h else slice(0, TOP_BWD)
        cols = slice(bwd_at[q], bwd_at[q] + BWD[q][0])
        total = colp[q][y, x, rows].astype(F32)
        for term in terms:
            total = total + term.astype(F32)
        gft[rows, cols] = (total + selfg[rows, cols]).astype(BF)

    def gradients(swaps):
        meet, when = links.start(dbias, dbias_in, partner, "core")
        yield swaps[-1][1]
        for copy, _ in swaps:
            copy.wait_recv()
        wide = WIDTH // 4
        for i in range(4):
            at = slice(i * wide, (i + 1) * wide)
            left = jnp.concatenate([lhs[k, :, at], lhs_in[:, at]], axis=0)
            both = jnp.concatenate([dlow[...], dlow_in[...]], axis=0)
            out = nn(left.T, both)
            for j in range(wide // DEEP):
                ez[i * (wide // DEEP) + j] = out[j * DEEP : (j + 1) * DEEP].astype(BF)
            plan.now += 0.4
            yield plan.now
        end = Join(2, lambda: plan.spawn(plane_sum(), plan.now))
        block, slot = cut(ez, DEEP // 2), cut(ez_in, DEEP // 2)
        for w, way in enumerate((1, -1)):
            plan.spawn(
                scatter_chain(
                    links,
                    "z",
                    way,
                    NZ,
                    z,
                    block,
                    lambda step, p, w=w: slot(w, step - 1, p),
                    at_z,
                    end.done,
                ),
                plan.now,
            )
        yield when
        meet.wait_recv()
        bz_in[z] = dbias[...] + dbias_in[...]
        bias_z.start()

    def plane_sum():
        yield plan.now
        bias_z.wait_recv()
        last = NZ // 2 - 1
        total = ez[z].astype(F32) + ez_in[0, last].astype(F32) + ez_in[1, last].astype(F32)
        low = bz_in[0]
        for i in range(1, NZ):
            low = low + bz_in[i]
        for j in range(NX):
            ex[j, 0:DEEP] = total[:, j * LANES : (j + 1) * LANES]
            ex[j, DEEP : DEEP + 8] = low
        ex_in[x] = ex[x]
        sum_x.start()
        yield plan.now + PLANE
        sum_x.wait_recv()
        total = ex_in[0]
        for i in range(1, NX):
            total = total + ex_in[i]
        for i in range(NY):
            ey[i, 0:8] = total[8 * i : 8 * i + 8]
            ey[i, 8:16] = total[DEEP : DEEP + 8]
        ey_in[y] = ey[y]
        sum_y.start()
        yield plan.now + PLANE
        sum_y.wait_recv()
        total = ey_in[0]
        for i in range(1, NY):
            total = total + ey_in[i]
        total = total * factor
        ag[y] = total[0:8]
        all_y.start()
        for j in range(WIDTH // LANES):
            gb[:, j * LANES : (j + 1) * LANES] = total[8 + j : 9 + j]
        yield plan.now + PLANE
        all_y.wait_recv()
        low = jnp.concatenate([ag[i] for i in range(NY)], axis=0).astype(BF)
        grads[k, z, :, lanes_of(x)] = low
        all_x.start()
        yield plan.now + PLANE
        all_x.wait_recv()
        mates = []
        end = Join(2, lambda: plan.spawn(collect(mates), max(when for _, when in mates)))
        view = cut(grads, DEEP // 2)

        def pass_on(o, p):
            ref = view(k, o, p)
            mates.append(links.start(ref, ref, partner, "core"))

        for way in (1, -1):
            chain = gather_chain(
                links,
                "z",
                way,
                NZ,
                z,
                lambda o, p: view(k, o, p),
                at_z,
                end.done,
                pass_on,
            )
            plan.spawn(chain, plan.now)

    def collect(mates):
        yield plan.now
        for copy, _ in mates:
            copy.wait_recv()

    factor = 1.0 / math.sqrt(ROWS * NR * NC)
    bias_z = Direct(links, NZ, z, at_z, lambda o: bz_in.at[z], lambda i: bz_in.at[i])
    sum_x = Direct(links, NX, x, at_x, lambda o: ex.at[o], lambda i: ex_in.at[i])
    sum_y = Direct(links, NY, y, at_y, lambda o: ey.at[o], lambda i: ey_in.at[i])
    all_y = Direct(links, NY, y, at_y, lambda o: ag.at[y], lambda i: ag.at[i])

    def lanes_of(i):
        return pl.ds(pl.multiple_of(i * LANES, LANES), LANES)

    all_x = Direct(
        links,
        NX,
        x,
        at_x,
        lambda o: grads.at[k, z, :, lanes_of(x)],
        lambda i: grads.at[k, z, :, lanes_of(i)],
    )

    ready_a = [Join(2 * (NX + NY), lambda q=q: plan.spawn(forward(q), plan.now)) for q in fwd]
    ready_b = Join(len(FWD), lambda: plan.spawn(middle(), plan.now))
    for q in fwd:
        plan.spawn(gather(q), STAGGER * q)
    plan.later(0.4, take_tiles)
    for m in range(SLOTS):
        plan.later(0.3, functools.partial(turn, m))
    plan.later(1.5, degrees)
    plan.later(1.0, self_term)
    plan.spawn(invert(), 2.0)
    plan.run()
    assert links.used <= SEMS

    stores = [
        pltpu.make_async_copy(gft, gfeat_out, local.at[16]),
        pltpu.make_async_copy(grads, grads_out, local.at[17]),
        pltpu.make_async_copy(gb, gbias_out, local.at[18]),
    ]
    for copy in stores:
        copy.start()
    links.finish()
    hidden_store.wait()
    for copy in stores:
        copy.wait()


def write_out(hidden, gfeat, grads, gbias, hidden_out, gfeat_out, gneigh_out, gself_out, gbias_out, *scratch):
    *held, sems = scratch
    sources = [grads.at[0], grads.at[1], hidden, gfeat, gbias]
    targets = [gneigh_out, gself_out, hidden_out, gfeat_out, gbias_out]
    count = len(held)
    takes = [pltpu.make_async_copy(a, b, sems.at[i]) for i, (a, b) in enumerate(zip(sources, held))]
    gives = [pltpu.make_async_copy(a, b, sems.at[count + i]) for i, (a, b) in enumerate(zip(held, targets))]
    for copy in takes:
        copy.start()
    for take, give in zip(takes, gives):
        take.wait()
        give.start()
    for copy in gives:
        copy.wait()


def on_device(
    features, tile_vals, tile_rows, tile_cols, tile_count, window, w_neigh, w_self, layer_bias, cotangent
):
    rows, width = features.shape
    slots, edge = tile_vals.shape[1:3]
    ny = lax.axis_size("row") // NX
    nz = lax.axis_size("col") // 2
    nc = 2 * nz

    def vmem(*shape, dtype=BF):
        return pltpu.VMEM(shape, dtype)

    fwd, bwd = [w for w, _ in FWD], [w for w, _ in BWD]
    each = [
        (fwd, (ny, NX, ROWS)),
        (fwd, (2, nz, ROWS)),
        (fwd, (nz, ROWS)),
        (fwd, (nz, ROWS)),
        (fwd, (slots + 1, edge)),
        (bwd, (nz, 2, ROWS)),
        (bwd, (slots + 1, edge)),
        (bwd, (ny, NX, ROWS)),
        (bwd, (2, ny // 2, NX, TOP_BWD)),
        (bwd, (NX, TOP_BWD)),
        (bwd, (2, NX // 2, ny, ROWS - TOP_BWD)),
        (bwd, (ny, ROWS - TOP_BWD)),
    ]
    deep = width // nz
    scratch = [vmem(*shape, w) for widths, shape in each for w in widths]
    scratch += [vmem(slots + 1, edge, edge)] * 2
    scratch += [vmem(rows, width), vmem(rows, width), vmem(width, width), vmem(width, width)]
    scratch += [vmem(1, width, dtype=F32)]
    scratch += [vmem(nc, 8, ROWS, dtype=F32)] * 2
    scratch += [vmem(ROWS, LANES, dtype=F32)] * 2
    scratch += [vmem(rows, width, dtype=F32)] * 2
    scratch += [vmem(2, rows, width), vmem(rows, width)]
    scratch += [vmem(rows, width)] * 2
    scratch += [vmem(8, LANES, dtype=F32)] * 2
    scratch += [vmem(nz, deep, width), vmem(2, nz // 2, deep, width)]
    scratch += [vmem(nz, 8, LANES, dtype=F32)]
    scratch += [vmem(NX, deep + 8, LANES, dtype=F32)] * 2
    scratch += [vmem(ny, 16, LANES, dtype=F32)] * 2
    scratch += [vmem(ny, 8, LANES, dtype=F32)]
    scratch += [vmem(2, nz, deep, width)]
    scratch += [vmem(rows, width)] * 2 + [vmem(1, width, dtype=F32)]
    scratch += [pltpu.SMEM(a.shape, jnp.int32) for a in (tile_rows, tile_cols, tile_count, window)]
    scratch += [pltpu.SemaphoreType.DMA((SEMS,))] * 2 + [pltpu.SemaphoreType.DMA((20,))]
    anywhere = pl.BlockSpec(memory_space=pl.ANY)
    far = pl.BlockSpec(memory_space=pltpu.HBM)
    sizes = (ny, nz, slots, edge, width)
    matrix = jax.ShapeDtypeStruct((rows, width), BF)
    weight = jax.ShapeDtypeStruct((nz, deep, width), BF)
    vector = jax.ShapeDtypeStruct((1, width), F32)
    results = pl.pallas_call(
        functools.partial(layer, sizes),
        out_shape=(matrix, matrix, jax.ShapeDtypeStruct((2, nz, deep, width), BF), vector),
        in_specs=[far] * 10,
        out_specs=(anywhere,) * 4,
        scratch_shapes=scratch,
        compiler_params=pltpu.CompilerParams(
            collective_id=0, has_side_effects=True, vmem_limit_bytes=VMEM_LIMIT
        ),
    )(
        features,
        tile_vals,
        tile_rows,
        tile_cols,
        tile_count,
        window,
        w_neigh,
        w_self,
        layer_bias.reshape(1, width),
        cotangent,
    )
    hidden, gfeat, gneigh, gself, gbias = pl.pallas_call(
        write_out,
        out_shape=(matrix, matrix, weight, weight, vector),
        in_specs=[anywhere] * 4,
        out_specs=(far,) * 5,
        scratch_shapes=[
            vmem(nz, deep, width),
            vmem(nz, deep, width),
            vmem(rows, width),
            vmem(rows, width),
            vmem(1, width, dtype=F32),
            pltpu.SemaphoreType.DMA((10,)),
        ],
        compiler_params=pltpu.CompilerParams(vmem_limit_bytes=VMEM_LIMIT),
    )(*results)
    return hidden, gfeat, gneigh.reshape(width, width), gself.reshape(width, width), gbias.reshape(width)


def solution(mesh):
    in_specs = (
        P(("col", "row"), None),
        P("row", "col", None, None),
        P("row", "col"),
        P("row", "col"),
        P("row", "col"),
        P("row", None),
        P(),
        P(),
        P(),
        P(("col", "row"), None),
    )
    out_specs = (P(("col", "row"), None), P(("col", "row"), None), P(), P(), P())
    return jax.shard_map(
        on_device, mesh=mesh, in_specs=in_specs, out_specs=out_specs, check_vma=False
    )
```
